256 devices in a mesh: batch: 8 (over z_hi, core), py: 8 (over x, z_lo), px: 4 (over y).
Axes of the slice: x: 4, y: 4, z: 8 (z_hi: 4, z_lo: 2; z = z_hi * 2 + z_lo), core: 2. Of those that a mesh axis runs over, the one named last changes fastest.
Arguments:
- latents: bfloat16 [512, 64, 1280], P(('batch', 'py'), 'px'), parts along dimension 0, may hold values from -30 to 30
- gn_gain: float32 [1280], replicated, may hold values from 0.25 to 1.75
- gn_bias: float32 [1280], replicated, may hold values from -3 to 3
- proj_weight: bfloat16 [1280, 1280], P(None, 'px'), may hold values from -0.15625 to 0.15625
- proj_bias: float32 [1280], replicated, may hold values from -3 to 3
- ln_gain: float32 [1280], replicated, may hold values from 0.25 to 1.75
- ln_bias: float32 [1280], replicated, may hold values from -3 to 3
- qkv_weight: bfloat16 [1280, 3840], P(None, 'px'), may hold values from -0.15625 to 0.15625
- stale_keys: bfloat16 [512, 64, 1280], P(('batch', 'py'), 'px'), parts along dimension 0, may hold values from -800 to 800
- stale_values: bfloat16 [512, 64, 1280], P(('batch', 'py'), 'px'), parts along dimension 0, may hold values from -6 to 6
Outputs:
- attended: bfloat16 [512, 64, 1280], P(('batch', 'py'), 'px'), parts along dimension 0
- fresh_keys: bfloat16 [512, 64, 1280], P(('batch', 'py'), 'px'), parts along dimension 0
- fresh_values: bfloat16 [512, 64, 1280], P(('batch', 'py'), 'px'), parts along dimension 0
The draws below stay inside these ranges and needn't reach their ends.
There are 8 independent parts, one for each index of `batch`. The reference program is written for one: setup_inputs(seed, part) draws one part's arguments, and reference() takes and returns one part's arrays. A program takes and returns all parts, laid end to end along the dimension named above; an argument that names none is the same for every part. Nothing has to cross between parts.
All inputs are finite; a program needn't handle non-finite values.
Results may differ from the reference program's by a relative error of at most 0.0272.
Values may be sent and summed in bfloat16 or wider, within the bound.
A program may use at most 128 MiB of HBM per device.

```python
import jax
import jax.numpy as jnp
from jax import lax

WIDTH = 1280
HEADS = 20
HEAD_DIM = 64
GROUPS = 32
PATCH_ROWS = 8
PATCH_COLS = 16
HEIGHT = 64
BREADTH = 64
N_PY = 8
N_PX = 4


def draw_latents(key, part):
    key = jax.random.fold_in(key, 11)
    key_noise, key_group, key_jitter, key_row, key_col = jax.random.split(key, 5)
    rows_pos = jnp.arange(HEIGHT, dtype=jnp.float32) / max(HEIGHT - 1, 1)
    cols_pos = jnp.arange(BREADTH, dtype=jnp.float32) / max(BREADTH - 1, 1)
    scale = jnp.exp(jnp.log(3.0) * 0.5 * (rows_pos[:, None] + cols_pos[None, :]))
    group_offset = jax.random.uniform(key_group, (GROUPS,), jnp.float32, -1.2, 1.2)
    jitter = jax.random.uniform(key_jitter, (WIDTH,), jnp.float32, -0.4, 0.4)
    channel_mean = jnp.repeat(group_offset, WIDTH // GROUPS) + jitter
    row_factor = jnp.exp(jax.random.uniform(key_row, (HEIGHT,), jnp.float32, jnp.log(0.3), jnp.log(1.5)))
    col_factor = jnp.exp(jax.random.uniform(key_col, (BREADTH,), jnp.float32, jnp.log(0.3), jnp.log(2.0)))
    noise = jnp.clip(jax.random.normal(key_noise, (HEIGHT, BREADTH, WIDTH), jnp.float32), -4.0, 4.0)
    region = row_factor[:, None] * col_factor[None, :]
    shifted = channel_mean[None, None, :] * region[:, :, None]
    return (scale[:, :, None] * (noise + shifted)).astype(jnp.bfloat16)


def draw_stale_keys(key, part):
    key = jax.random.fold_in(key, 23)
    base = jnp.clip(jax.random.normal(key, (HEIGHT * BREADTH, WIDTH), jnp.float32), -5.0, 5.0)
    return base.reshape(HEIGHT, BREADTH, WIDTH).astype(jnp.bfloat16)


def shard_levels(own_key, dims, cuts, least, top_value):
    factor_of = 1.0
    for dim, shards_of in cuts:
        draws = jax.random.uniform(jax.random.fold_in(jax.random.fold_in(own_key, 6), dim), (shards_of,), jnp.float32, least / len(cuts), top_value / len(cuts))
        factor_of = factor_of * jnp.repeat(jnp.exp(draws), dims[dim] // shards_of).reshape((-1,) + (1,) * (len(dims) - 1 - dim))
    return factor_of


def scatter_about(key, shape, deviation, most, pieces=(), kind=jnp.bfloat16):
    entries = jax.random.normal(key, shape, jnp.float32) * deviation
    if len(pieces) > 0:
        entries = shard_levels(key, shape, pieces, -0.22, 0.18) * entries
    return jnp.clip(entries, min=-most, max=most).astype(kind)


def setup_inputs(seed: int = 0, part: int = 0) -> dict:
    key_list = jax.random.split(jax.random.key(seed), 11)
    own_keys = jax.random.split(jax.random.fold_in(key_list[10], part), 11)
    return {
        "latents": draw_latents(jax.random.fold_in(jax.random.fold_in(key_list[10], part), 71), part),
        "gn_gain": jnp.clip(1.0 + 0.15 * jax.random.normal(key_list[1], (WIDTH,), jnp.float32), 0.25, 1.75),
        "gn_bias": scatter_about(key_list[2], (WIDTH,), 0.5, 3.0, (), jnp.float32),
        "proj_weight": scatter_about(key_list[3], (WIDTH, WIDTH), WIDTH ** -0.5, 0.15625, ((1, 4),)),
        "proj_bias": scatter_about(key_list[4], (WIDTH,), 0.5, 3.0, (), jnp.float32),
        "ln_gain": jnp.clip(1.0 + 0.15 * jax.random.normal(key_list[5], (WIDTH,), jnp.float32), 0.25, 1.75),
        "ln_bias": scatter_about(key_list[6], (WIDTH,), 0.5, 3.0, (), jnp.float32),
        "qkv_weight": scatter_about(key_list[7], (WIDTH, 3 * WIDTH), WIDTH ** -0.5, 0.15625, ((1, 4),)),
        "stale_keys": draw_stale_keys(jax.random.fold_in(jax.random.fold_in(key_list[10], part), 71), part),
        "stale_values": scatter_about(own_keys[9], (HEIGHT, BREADTH, WIDTH), 1.0, 6.0, ((0, 8), (1, 4))),
    }


def to_patches(field):
    width = field.shape[-1]
    shaped = field.reshape(N_PY, PATCH_ROWS, N_PX, PATCH_COLS, width)
    return shaped.transpose(0, 2, 1, 3, 4).reshape(N_PY * N_PX, PATCH_ROWS * PATCH_COLS, width)

def from_patches(field):
    width = field.shape[-1]
    shaped = field.reshape(N_PY, N_PX, PATCH_ROWS, PATCH_COLS, width)
    return shaped.transpose(0, 2, 1, 3, 4).reshape(N_PY * PATCH_ROWS, N_PX * PATCH_COLS, width)

def reference(latents, gn_gain, gn_bias, proj_weight, proj_bias, ln_gain, ln_bias, qkv_weight, stale_keys, stale_values):
    height, breadth, width = latents.shape
    count_tok = height * breadth
    values_in = latents.astype(jnp.float32).reshape(count_tok, GROUPS, width // GROUPS)
    mean = lax.optimization_barrier(jnp.mean(values_in, axis=(0, 2), keepdims=True))
    spread = lax.optimization_barrier(jnp.mean((values_in - mean) ** 2, axis=(0, 2), keepdims=True))
    grouped = ((values_in - mean) * lax.rsqrt(spread + 1e-06)).reshape(count_tok, width)
    grouped = (grouped * gn_gain + gn_bias).astype(jnp.bfloat16)
    projected = jnp.dot(grouped, proj_weight, preferred_element_type=jnp.float32) + proj_bias
    row_mean = lax.optimization_barrier(jnp.mean(projected, axis=-1, keepdims=True))
    row_var = lax.optimization_barrier(jnp.mean((projected - row_mean) ** 2, axis=-1, keepdims=True))
    normed = ((projected - row_mean) * lax.rsqrt(row_var + 1e-05) * ln_gain + ln_bias).astype(jnp.bfloat16)
    qkv = jnp.dot(normed, qkv_weight, preferred_element_type=jnp.float32)
    queries = qkv[:, :width].astype(jnp.bfloat16).reshape(height, breadth, width)
    fresh_keys = qkv[:, width:2 * width].astype(jnp.bfloat16).reshape(height, breadth, width)
    fresh_values = qkv[:, 2 * width:].astype(jnp.bfloat16).reshape(height, breadth, width)
    query_p = to_patches(queries)
    key_p = to_patches(fresh_keys)
    value_p = to_patches(fresh_values)
    all_keys = to_patches(stale_keys).reshape(-1, HEADS, HEAD_DIM).astype(jnp.float32)
    all_values = to_patches(stale_values).reshape(-1, HEADS, HEAD_DIM).astype(jnp.float32)
    tok_p = PATCH_ROWS * PATCH_COLS
    total_keys = all_keys.shape[0]
    owner = (jnp.arange(total_keys, dtype=jnp.int32) // tok_p).astype(jnp.int32)
    factor = HEAD_DIM ** (-0.5)

    def one_patch(index):
        query = query_p[index].reshape(tok_p, HEADS, HEAD_DIM).astype(jnp.float32)
        own_k = key_p[index].reshape(tok_p, HEADS, HEAD_DIM).astype(jnp.float32)
        own_v = value_p[index].reshape(tok_p, HEADS, HEAD_DIM).astype(jnp.float32)
        score_all = jnp.einsum('qhd,khd->hqk', query, all_keys) * factor
        score_all = jnp.where((owner == index)[None, None, :], -1e+30, score_all)
        score_own = jnp.einsum('qhd,khd->hqk', query, own_k) * factor
        top = jnp.maximum(lax.optimization_barrier(jnp.max(score_all, axis=-1)), lax.optimization_barrier(jnp.max(score_own, axis=-1)))
        exp_all = jnp.exp(score_all - top[..., None])
        exp_own = jnp.exp(score_own - top[..., None])
        total = lax.optimization_barrier(jnp.sum(exp_all, axis=-1)) + lax.optimization_barrier(jnp.sum(exp_own, axis=-1))
        weight_all = exp_all.astype(jnp.bfloat16).astype(jnp.float32)
        weight_own = exp_own.astype(jnp.bfloat16).astype(jnp.float32)
        summed = jnp.einsum('hqk,khd->hqd', weight_all, all_values) + jnp.einsum('hqk,khd->hqd', weight_own, own_v)
        result = summed / total[..., None]
        return result.transpose(1, 0, 2).reshape(tok_p, HEADS * HEAD_DIM)
    outputs = lax.map(one_patch, jnp.arange(N_PY * N_PX, dtype=jnp.int32))
    attended = from_patches(outputs).astype(jnp.bfloat16)
    return (attended, fresh_keys, fresh_values)
```

```python
import jax
import jax.numpy as jnp
from jax import lax
from jax.experimental import pallas as pl
from jax.experimental.pallas import tpu as pltpu
from jax.sharding import PartitionSpec as P

MESH = pl.DeviceIdType.MESH
HIGHEST = lax.Precision.HIGHEST
BF16 = jnp.bfloat16
F32 = jnp.float32

WIDTH = 1280
HEADS = 20
HEAD_DIM = 64
GROUPS = 32
N_PY = 8
N_PX = 4
TOK = 128
GROUP_HEADS = HEADS // N_PX
COLS = WIDTH // N_PX
PAIR = GROUP_HEADS * 2 * HEAD_DIM
ENTRIES = TOK * (WIDTH // GROUPS)

SLOTS = ((0, 0), (0, 1), (1, 0), (3, 0), (1, 1), (3, 1), (2, 0), (2, 1))


def slot_of(dx, dz):
    return SLOTS.index((dx % 4, dz))


def mm(a, b, precision=None):
    return lax.dot_general(
        a, b, (((1,), (0,)), ((), ())), precision=precision, preferred_element_type=F32
    )


def mm_t(a, b, precision=None):
    return lax.dot_general(
        a, b, (((1,), (1,)), ((), ())), precision=precision, preferred_element_type=F32
    )


def merge(means, squares, count):
    n = len(means)
    mean = sum(means[1:], means[0]) * (1.0 / n)
    total = sum(squares[1:], squares[0])
    for part in means:
        total = total + count * (part - mean) * (part - mean)
    return mean, total


def kernel(
    lat_ref, gng_ref, gnb_ref, pw_ref, pb_ref, lng_ref, lnb_ref, qw_ref, sk_ref, sv_ref,
    att_ref, fk_ref, fv_ref,
    latg, st_out, st_py, st_mid, st_px, proj, ln_out, ln_in, nrm_a, nrm_b,
    wst, wrecv, wa, wb, qkv_acc, q_buf, fkv, frecv, kvs, kvg, acc, top, ost, orecv,
    lat_s, lat_r, sp_s, sp_r, sx_s, sx_r, ln_s, ln_r, na_s, na_r, nb_s, nb_r,
    w1_s, w1_r, w2_s, w2_r, ky_s, kx_s, kf_s, kv_r, fr_s, fr_r, or_s, or_r,
):
    b = lax.axis_index("batch")
    p = lax.axis_index("py")
    j = lax.axis_index("px")
    core = lax.rem(b, 2)
    x, z_lo = p // 2, lax.rem(p, 2)
    quarter = 2 * z_lo + core

    px_peer = [(j + k) % N_PX for k in range(N_PX)]
    px_id = [(b, p, t) for t in px_peer]
    py_id = [(b, lax.rem(x + dx, 4) * 2 + (z_lo if dz == 0 else 1 - z_lo), j) for dx, dz in SLOTS]
    other_b = lax.rem(b + jnp.where(z_lo == 1, 2, 6), 8)
    swap = 1 - 2 * core
    copies_id = [(b + swap, p, j), (other_b, p + 1 - 2 * z_lo, j), (other_b + swap, p + 1 - 2 * z_lo, j)]
    copies_q = [2 * z_lo + 1 - core, 2 * (1 - z_lo) + core, 2 * (1 - z_lo) + 1 - core]

    barrier = pltpu.get_barrier_semaphore()
    peers = px_id[1:] + py_id[1:] + copies_id
    for peer in peers:
        pl.semaphore_signal(barrier, inc=1, device_id=peer, device_id_type=MESH)

    sends = []

    def send(src, dst, s_sem, r_sem, peer):
        copy = pltpu.make_async_remote_copy(
            src_ref=src, dst_ref=dst, send_sem=s_sem, recv_sem=r_sem,
            device_id=peer, device_id_type=MESH,
        )
        copy.start()
        sends.append(copy)

    def received(dst, r_sem):
        pltpu.make_async_remote_copy(
            src_ref=dst, dst_ref=dst, send_sem=lat_s.at[0], recv_sem=r_sem,
            device_id=px_id[1], device_id_type=MESH,
        ).wait_recv()

    for t in range(N_PX):
        for h in range(GROUP_HEADS):
            lanes = slice((t * GROUP_HEADS + h) * HEAD_DIM, (t * GROUP_HEADS + h + 1) * HEAD_DIM)
            kvs[t, :, h * 128 : (h + 1) * 128] = jnp.concatenate(
                [sk_ref[:, lanes], sv_ref[:, lanes]], axis=1
            )

    chan = lax.broadcasted_iota(jnp.int32, (WIDTH, 128), 0)
    group = lax.broadcasted_iota(jnp.int32, (WIDTH, 128), 1) * (WIDTH // GROUPS)
    member = jnp.where((chan >= group) & (chan < group + WIDTH // GROUPS), 1.0, 0.0).astype(F32)

    def to_groups(row):
        return mm(jnp.broadcast_to(row, (8, WIDTH)), member, HIGHEST)

    def to_channels(row):
        return mm_t(row, member, HIGHEST)[0:1]

    own = lat_ref[...].astype(F32)
    own_mean = to_groups(jnp.sum(own, axis=0, keepdims=True)) * (1.0 / ENTRIES)
    centered = own - to_channels(own_mean)
    own_squares = to_groups(jnp.sum(centered * centered, axis=0, keepdims=True))
    st_out[0:8] = own_mean
    st_out[8:16] = own_squares
    st_py[0] = st_out[...]

    pl.semaphore_wait(barrier, len(peers))

    for i in range(1, 8):
        dx, dz = SLOTS[i]
        send(st_out, st_py.at[slot_of(-dx, dz)], sp_s.at[i], sp_r.at[slot_of(-dx, dz)], py_id[i])
    for k in range(1, 4):
        send(lat_ref, latg.at[j], lat_s.at[k], lat_r.at[j], px_id[k])
    for k in range(1, 4):
        send(kvs.at[px_peer[k]], kvg.at[0, j], ky_s.at[k], kv_r.at[0, j], px_id[k])

    def spread(unit, src, k):
        for i in range(1, 8):
            dx, dz = SLOTS[i]
            there = slot_of(-dx, dz)
            send(src, kvg.at[there, unit], kx_s.at[k, i], kv_r.at[there, unit], py_id[i])

    spread(j, kvs.at[j], 0)
    kvg[0, j] = kvs[j]

    rows = qw_ref[pl.ds(pl.multiple_of(quarter * COLS, 64), COLS), :]
    for s in range(3):
        wst[s, :, 0:COLS] = rows[:, s * COLS : (s + 1) * COLS]
    even = lax.rem(j, 2) == 0
    kind_own = jnp.where(j == 0, 0, jnp.where(j == 3, 2, 1))
    kind_1 = jnp.where(j == 0, 1, 0)
    kind_2 = jnp.where(j == 3, 1, 2)
    for d in range(N_PX):
        part = slice(d * COLS, (d + 1) * COLS)
        wrecv[kind_own, d, :, 0:COLS] = jnp.where(even, qw_ref[part, 0:COLS], qw_ref[part, 2 * COLS :])

    for i in range(1, 8):
        received(st_py.at[i], sp_r.at[i])
    mean, squares = merge(
        [st_py[i, 0:8] for i in range(8)], [st_py[i, 8:16] for i in range(8)], float(ENTRIES)
    )
    st_mid[0:8] = mean
    st_mid[8:16] = squares
    st_px[j] = st_mid[...]
    for k in range(1, 4):
        send(st_mid, st_px.at[j], sx_s.at[k], sx_r.at[j], px_id[k])
    for k in range(1, 4):
        received(st_px.at[px_peer[k]], sx_r.at[px_peer[k]])
    mean, squares = merge(
        [st_px[i, 0:8] for i in range(4)], [st_px[i, 8:16] for i in range(4)], float(ENTRIES * 8)
    )
    spread_all = squares * (1.0 / (ENTRIES * 32))
    gn_mean = to_channels(mean)
    gn_scale = to_channels(lax.rsqrt(spread_all + 1e-06)) * gng_ref[...]
    gn_shift = gnb_ref[...]

    def own_columns(ref):
        out = ref[:, 0:COLS]
        for t in range(1, N_PX):
            out = jnp.where(j == t, ref[:, t * COLS : (t + 1) * COLS], out)
        return out

    proj_bias = own_columns(pb_ref)
    ones = jnp.ones((8, COLS), F32)
    row8 = lax.broadcasted_iota(jnp.int32, (8, TOK), 0)

    def project(t, source):
        grouped = ((source[...].astype(F32) - gn_mean) * gn_scale + gn_shift).astype(BF16)
        out = mm(grouped, pw_ref[...]) + proj_bias
        proj[t] = out
        off = out - jnp.sum(out, axis=1, keepdims=True) * (1.0 / COLS)
        part_mean = mm_t(ones, out, HIGHEST) * (1.0 / COLS)
        part_squares = mm_t(ones, off * off, HIGHEST)
        ln_out[t] = jnp.where(row8 < 4, part_mean, part_squares)

    project(j, lat_ref)
    for k in range(1, 4):
        received(latg.at[px_peer[k]], lat_r.at[px_peer[k]])
        project(px_peer[k], latg.at[px_peer[k]])

    for k in range(1, 4):
        send(ln_out, ln_in.at[j], ln_s.at[k], ln_r.at[j], px_id[k])
    ln_in[j] = ln_out[...]

    slot_1 = jnp.where(even, 1, 0)
    for i in range(2):
        block = 3 * j + slot_1 + i
        send(
            wst.at[slot_1 + i], wrecv.at[block // 4, quarter],
            w1_s.at[i], w1_r.at[block // 4], (b, p, lax.rem(block, 4)),
        )
    for k in range(1, 4):
        received(kvg.at[0, px_peer[k]], kv_r.at[0, px_peer[k]])
        spread(px_peer[k], kvg.at[0, px_peer[k]], k)

    ln_gain = own_columns(lng_ref)
    ln_bias = own_columns(lnb_ref)
    for k in range(1, 4):
        received(ln_in.at[px_peer[k]], ln_r.at[px_peer[k]])
    tails = []
    for t in range(N_PX):
        mean, squares = merge(
            [ln_in[d, t, 0:1] for d in range(N_PX)], [ln_in[d, t, 4:5] for d in range(N_PX)], float(COLS)
        )
        scale = lax.rsqrt(squares * (1.0 / WIDTH) + 1e-05)
        both = jnp.where(row8 < 4, jnp.broadcast_to(mean, (8, TOK)), jnp.broadcast_to(scale, (8, TOK)))
        both = both.T
        normed = ((proj[t] - both[:, 0:1]) * both[:, 4:5] * ln_gain + ln_bias).astype(BF16)
        nrm_a[j, t * TOK : (t + 1) * TOK] = normed[:, 0:256]
        tails.append(normed[:, 256:COLS])
    for i in range(2):
        nrm_b[j, i] = jnp.concatenate([tails[i], tails[i + 2]], axis=1)
    for k in range(1, 4):
        send(nrm_a.at[j], nrm_a.at[j], na_s.at[k], na_r.at[j], px_id[k])
        send(nrm_b.at[j], nrm_b.at[j], nb_s.at[k], nb_r.at[j], px_id[k])

    for i, kind in enumerate((kind_1, kind_2)):
        received(wrecv.at[kind, quarter], w1_r.at[kind])
        for c in range(3):
            send(wrecv.at[kind, quarter], wrecv.at[kind, quarter], w2_s.at[i, c], w2_r.at[i, quarter], copies_id[c])
    for i, kind in enumerate((kind_1, kind_2)):
        for c in range(3):
            received(wrecv.at[kind, copies_q[c]], w2_r.at[i, copies_q[c]])
    blank = jnp.zeros((COLS, HEAD_DIM), BF16)
    for d in range(N_PX):
        for h in range(GROUP_HEADS):
            lanes = slice(h * HEAD_DIM, (h + 1) * HEAD_DIM)
            query = jnp.concatenate([wrecv[0, d, :, lanes], blank], axis=1)
            pair = jnp.concatenate([wrecv[1, d, :, lanes], wrecv[2, d, :, lanes]], axis=1)
            for value, start in ((query, h * 128), (pair, PAIR + h * 128)):
                wa[d, :, start : start + 128] = value[0:256]
                wb[d * 64 : (d + 1) * 64, start : start + 128] = value[256:COLS]

    qkv_acc[...] = mm(nrm_a[j], wa[j])
    for k in range(1, 4):
        d = px_peer[k]
        received(nrm_a.at[d], na_r.at[d])
        qkv_acc[...] += mm(nrm_a[d], wa[d])
    for k in range(1, 4):
        received(nrm_b.at[px_peer[k]], nb_r.at[px_peer[k]])
    tail = jnp.concatenate(
        [
            jnp.concatenate([nrm_b[d, i, :, half * 64 : half * 64 + 64] for d in range(N_PX)], axis=1)
            for half in range(2)
            for i in range(2)
        ],
        axis=0,
    )
    qkv = qkv_acc[...] + mm(tail, wb[...])
    for t in range(N_PX):
        token = slice(t * TOK, (t + 1) * TOK)
        q_buf[t] = (qkv[token, 0:PAIR] * HEAD_DIM ** (-0.5)).astype(BF16)
        fkv[t] = qkv[token, PAIR:].astype(BF16)
    for k in range(1, 4):
        send(fkv.at[px_peer[k]], frecv.at[j], fr_s.at[k], fr_r.at[j], px_id[k])
    frecv[j] = fkv[j]

    for i in range(1, 4):
        for u in range(N_PX):
            received(kvg.at[i, u], kv_r.at[i, u])
    lane = lax.broadcasted_iota(jnp.int32, (2048, 128), 1)

    def head_lanes(h):
        return slice(h * 128, (h + 1) * 128)

    def first_keys(h, t):
        lanes = head_lanes(h)
        parts = [fkv[t, :, lanes] if u == t else kvg[0, u, :, lanes] for u in range(N_PX)]
        parts.append(kvg[1:4, :, :, lanes].reshape(1536, 128))
        return jnp.concatenate(parts, axis=0)

    def second_keys(h, t):
        return kvg[4:8, :, :, head_lanes(h)].reshape(2048, 128)

    def weigh(weight, keys):
        return mm(weight.astype(BF16), jnp.where(lane < HEAD_DIM, jnp.ones((), BF16), keys))

    items = [(h, t) for t in range(N_PX) for h in range(GROUP_HEADS)]
    score = mm_t(q_buf[items[0][1], :, head_lanes(items[0][0])], first_keys(*items[0]))
    for n, (h, t) in enumerate(items):
        following = None
        if n + 1 < len(items):
            h2, t2 = items[n + 1]
            following = mm_t(q_buf[t2, :, head_lanes(h2)], first_keys(h2, t2))
        new = jnp.max(score, axis=1, keepdims=True)
        weight = jnp.exp(score - new)
        top[h, t] = jnp.broadcast_to(new, (TOK, 128))
        acc[h, t] = weigh(weight, first_keys(h, t))
        score = following

    for i in range(4, 8):
        for u in range(N_PX):
            received(kvg.at[i, u], kv_r.at[i, u])
    order = [px_peer[1], px_peer[2], px_peer[3], j]
    items = [(h, k) for k in range(N_PX) for h in range(GROUP_HEADS)]
    score = mm_t(q_buf[order[0], :, head_lanes(0)], second_keys(0, 0))
    outs = []
    for n, (h, k) in enumerate(items):
        following = None
        if n + 1 < len(items):
            h2, k2 = items[n + 1]
            following = mm_t(q_buf[order[k2], :, head_lanes(h2)], second_keys(h2, k2))
        t = order[k]
        old = top[h, t]
        new = jnp.maximum(old, jnp.max(score, axis=1, keepdims=True))
        weight = jnp.exp(score - new[:, 0:1])
        total = acc[h, t] * jnp.exp(old - new) + weigh(weight, second_keys(h, k))
        outs.append(total[:, HEAD_DIM:] / total[:, 0:HEAD_DIM])
        if h == GROUP_HEADS - 1:
            target = ost if k < 3 else orecv
            slot = k if k < 3 else j
            outs.append(jnp.zeros((TOK, HEAD_DIM), F32))
            target[slot] = jnp.concatenate(outs, axis=1).astype(BF16)
            outs = []
            if k < 3:
                send(ost.at[k], orecv.at[j], or_s.at[k], or_r.at[j], px_id[k + 1])
        score = following

    for k in range(1, 4):
        received(frecv.at[px_peer[k]], fr_r.at[px_peer[k]])
    for first, out_ref in ((0, fk_ref), (HEAD_DIM, fv_ref)):
        out_ref[...] = jnp.concatenate(
            [
                frecv[g, :, h * 128 + first : h * 128 + first + HEAD_DIM]
                for g in range(N_PX)
                for h in range(GROUP_HEADS)
            ],
            axis=1,
        )
    for k in range(1, 4):
        received(orecv.at[px_peer[k]], or_r.at[px_peer[k]])
    att_ref[...] = jnp.concatenate([orecv[g, :, 0:COLS] for g in range(N_PX)], axis=1)
    for copy in sends:
        copy.wait_send()


def shards(
    latents, gn_gain, gn_bias, proj_weight, proj_bias, ln_gain, ln_bias, qkv_weight, stale_keys, stale_values
):
    patch_rows, patch_cols, width = latents.shape
    tokens = patch_rows * patch_cols
    dma = pltpu.SemaphoreType.DMA
    vmem = pl.BlockSpec(memory_space=pltpu.VMEM)
    out = jax.ShapeDtypeStruct((tokens, width), BF16)
    scratch = [
        pltpu.VMEM((N_PX, TOK, WIDTH), BF16),
        pltpu.VMEM((16, 128), F32),
        pltpu.VMEM((N_PY, 16, 128), F32),
        pltpu.VMEM((16, 128), F32),
        pltpu.VMEM((N_PX, 16, 128), F32),
        pltpu.VMEM((N_PX, TOK, COLS), F32),
        pltpu.VMEM((N_PX, 8, TOK), F32),
        pltpu.VMEM((N_PX, N_PX, 8, TOK), F32),
        pltpu.VMEM((N_PX, 4 * TOK, 256), BF16),
        pltpu.VMEM((N_PX, 2, TOK, 128), BF16),
        pltpu.VMEM((3, COLS, 384), BF16),
        pltpu.VMEM((3, N_PX, COLS, 384), BF16),
        pltpu.VMEM((N_PX, 256, 2 * PAIR), BF16),
        pltpu.VMEM((256, 2 * PAIR), BF16),
        pltpu.VMEM((4 * TOK, 2 * PAIR), F32),
        pltpu.VMEM((N_PX, TOK, PAIR), BF16),
        pltpu.VMEM((N_PX, TOK, PAIR), BF16),
        pltpu.VMEM((N_PX, TOK, PAIR), BF16),
        pltpu.VMEM((N_PX, TOK, PAIR), BF16),
        pltpu.VMEM((N_PY, N_PX, TOK, PAIR), BF16),
        pltpu.VMEM((GROUP_HEADS, N_PX, TOK, 128), F32),
        pltpu.VMEM((GROUP_HEADS, N_PX, TOK, 128), F32),
        pltpu.VMEM((3, TOK, 384), BF16),
        pltpu.VMEM((N_PX, TOK, 384), BF16),
    ]
    sems = [
        (4,), (4,), (8,), (8,), (4,), (4,), (4,), (4,), (4,), (4,), (4,), (4,),
        (2,), (3,), (2, 3), (2, 4), (4,), (4, 8), (1,), (8, 4), (4,), (4,), (4,), (4,),
    ]
    attended, fresh_keys, fresh_values = pl.pallas_call(
        kernel,
        out_shape=(out, out, out),
        in_specs=[vmem] * 10,
        out_specs=(vmem, vmem, vmem),
        scratch_shapes=scratch + [dma(shape) for shape in sems],
        compiler_params=pltpu.CompilerParams(
            collective_id=0, has_side_effects=True, vmem_limit_bytes=56 * 1024 * 1024
        ),
        name="patch_attention",
    )(
        latents.reshape(tokens, width),
        gn_gain.reshape(1, width), gn_bias.reshape(1, width),
        proj_weight, proj_bias.reshape(1, width),
        ln_gain.reshape(1, width), ln_bias.reshape(1, width),
        qkv_weight,
        stale_keys.reshape(tokens, width), stale_values.reshape(tokens, width),
    )
    shape = (patch_rows, patch_cols, width)
    return attended.reshape(shape), fresh_keys.reshape(shape), fresh_values.reshape(shape)


def solution(mesh):
    split = P(("batch", "py"), "px", None)
    return jax.shard_map(
        shards,
        mesh=mesh,
        in_specs=(split, P(), P(), P(None, "px"), P(), P(), P(), P(None, "px"), split, split),
        out_specs=(split, split, split),
        check_vma=False,
    )
```

```python
import jax
import jax.numpy as jnp
from jax import lax
from jax.experimental import pallas as pl
from jax.experimental.pallas import tpu as pltpu
from jax.sharding import PartitionSpec as P

MESH = pl.DeviceIdType.MESH
HIGHEST = lax.Precision.HIGHEST
BF16 = jnp.bfloat16
F32 = jnp.float32

WIDTH = 1280
HEADS = 20
HEAD_DIM = 64
GROUPS = 32
N_PY = 8
N_PX = 4
TOK = 128
GROUP_HEADS = HEADS // N_PX
COLS = WIDTH // N_PX
QUARTER = COLS // 4
PAIR = GROUP_HEADS * 2 * HEAD_DIM
ENTRIES = TOK * (WIDTH // GROUPS)

SLOTS = ((0, 0), (0, 1), (1, 0), (3, 0), (1, 1), (3, 1), (2, 0), (2, 1))


def slot_of(dx, dz):
    return SLOTS.index((dx % 4, dz))


def mm(a, b, precision=None):
    return lax.dot_general(
        a, b, (((1,), (0,)), ((), ())), precision=precision, preferred_element_type=F32
    )


def mm_t(a, b, precision=None):
    return lax.dot_general(
        a, b, (((1,), (1,)), ((), ())), precision=precision, preferred_element_type=F32
    )


def merge(means, squares, count):
    n = len(means)
    mean = sum(means[1:], means[0]) * (1.0 / n)
    total = sum(squares[1:], squares[0])
    for part in means:
        total = total + count * (part - mean) * (part - mean)
    return mean, total


def kernel(
    lat_hbm, gng_ref, gnb_ref, pw_hbm, pb_ref, lng_ref, lnb_ref, qw_hbm, sk_hbm, sv_hbm,
    fresh_out, att_out,
    lat_ref, sk_ref, sv_ref, pw_ref, latg, st_out, st_py, st_mid, st_px, proj, ln_out, ln_in, nrm,
    wq, qkv_acc, q_buf, fkv, kvs, kvg, acc, top, ost,
    load_s, send_s, lat_r, sp_r, sx_r, ln_r, nrm_r, w_r, kv_r, fr_r, or_r,
):
    b = lax.axis_index("batch")
    p = lax.axis_index("py")
    j = lax.axis_index("px")
    core = lax.rem(b, 2)
    x, z_lo = p // 2, lax.rem(p, 2)
    x_odd = lax.rem(x, 2) == 1
    even = lax.rem(j, 2) == 0

    px_peer = [(j + k) % N_PX for k in range(N_PX)]
    px_id = [(b, p, t) for t in px_peer]
    py_id = [(b, lax.rem(x + dx, 4) * 2 + (z_lo if dz == 0 else 1 - z_lo), j) for dx, dz in SLOTS]
    core_id = (b + 1 - 2 * core, p, j)
    across_id = (lax.rem(b + jnp.where(z_lo == 1, 2, 6), 8), p + 1 - 2 * z_lo, j)
    x_pair_id = (b, p + 2 - 4 * lax.rem(x, 2), j)

    own_slot = jnp.where(even, 0, 2)
    kind_own = jnp.where(j == 0, 0, jnp.where(j == 3, 2, 1))
    loads = [
        pltpu.make_async_copy(src, dst, load_s.at[i])
        for i, (src, dst) in enumerate(
            (
                (lat_hbm, lat_ref), (sk_hbm, sk_ref), (sv_hbm, sv_ref), (pw_hbm, pw_ref),
                (qw_hbm.at[pl.ds(pl.multiple_of(own_slot * COLS, 16), COLS)], wq.at[kind_own]),
            )
        )
    ]
    for load in loads:
        load.start()

    barrier = pltpu.get_barrier_semaphore()
    peers = px_id[1:] + py_id[1:] + [core_id, across_id]
    for peer in peers:
        pl.semaphore_signal(barrier, inc=1, device_id=peer, device_id_type=MESH)
    pl.semaphore_wait(barrier, len(peers))

    sends = []

    def send(src, dst, r_sem, peer):
        copy = pltpu.make_async_remote_copy(
            src_ref=src, dst_ref=dst, send_sem=send_s.at[len(sends)], recv_sem=r_sem,
            device_id=peer, device_id_type=MESH,
        )
        copy.start()
        sends.append(copy)

    def received(dst, r_sem):
        pltpu.make_async_remote_copy(
            src_ref=dst, dst_ref=dst, send_sem=send_s.at[0], recv_sem=r_sem,
            device_id=px_id[1], device_id_type=MESH,
        ).wait_recv()

    halves = (pl.ds(0, TOK // 2), pl.ds(TOK // 2, TOK // 2))

    for half in range(2):
        for k, own_half in ((1, half), (3, 1 - half)):
            rows = halves[own_half]
            send(lat_hbm.at[rows], latg.at[j, rows], lat_r.at[j, own_half], px_id[k])

    def lat_received(k, half):
        t = px_peer[k]
        received(latg.at[t, halves[half]], lat_r.at[t, half])

    def lat_forward(k, half):
        t = px_peer[k]
        lat_received(k, half)
        rows = halves[half]
        send(latg.at[t, rows], latg.at[t, rows], lat_r.at[t, half], px_id[4 - k])

    chan = lax.broadcasted_iota(jnp.int32, (WIDTH, 128), 0)
    group = lax.broadcasted_iota(jnp.int32, (WIDTH, 128), 1) * (WIDTH // GROUPS)
    member = jnp.where((chan >= group) & (chan < group + WIDTH // GROUPS), 1.0, 0.0).astype(F32)

    def to_groups(row):
        return mm(jnp.broadcast_to(row, (8, WIDTH)), member, HIGHEST)

    def to_channels(row):
        return mm_t(row, member, HIGHEST)[0:1]

    loads[0].wait()
    own = lat_ref[...].astype(F32)
    own_mean = to_groups(jnp.sum(own, axis=0, keepdims=True)) * (1.0 / ENTRIES)
    centered = own - to_channels(own_mean)
    own_squares = to_groups(jnp.sum(centered * centered, axis=0, keepdims=True))
    st_out[0:8] = own_mean
    st_out[8:16] = own_squares
    st_py[0] = st_out[...]
    for i in range(1, 8):
        dx, dz = SLOTS[i]
        send(st_out, st_py.at[slot_of(-dx, dz)], sp_r.at[slot_of(-dx, dz)], py_id[i])

    loads[1].wait()
    loads[2].wait()
    for t in range(N_PX):
        for h in range(GROUP_HEADS):
            lanes = slice((t * GROUP_HEADS + h) * HEAD_DIM, (t * GROUP_HEADS + h + 1) * HEAD_DIM)
            kvs[t, :, h * 128 : (h + 1) * 128] = jnp.concatenate(
                [sk_ref[:, lanes], sv_ref[:, lanes]], axis=1
            )
    kvg[0, j] = kvs[j]

    kv_done = set()

    def kv_received(slot, k):
        if (slot, k) not in kv_done:
            kv_done.add((slot, k))
            received(kvg.at[slot, px_peer[k]], kv_r.at[slot, px_peer[k]])

    def kv_send(slot, k, to_slot, peer):
        u = px_peer[k]
        send(kvg.at[slot, u], kvg.at[to_slot, u], kv_r.at[to_slot, u], peer)

    def kv_sides(z, k):
        for dx in (1, 3):
            kv_send(z, k, slot_of(-dx, z), py_id[slot_of(dx, 0)])

    def kv_first(k):
        kv_send(0, k, 1, py_id[1])
        kv_sides(0, k)

    def kv_opposite(z, k):
        dx = 3 if k % 2 == 0 else 1
        kv_received(slot_of(dx, z), k)
        kv_send(slot_of(dx, z), k, slot_of(2, z), py_id[slot_of(-dx, 0)])

    def kv_second(k):
        kv_received(1, k)
        kv_sides(1, k)

    def kv_across(dx, k):
        kv_received(slot_of(dx, 0), k)
        kv_send(slot_of(dx, 0), k, slot_of(dx, 1), py_id[1])

    kv_first(0)
    lat_forward(3, 0)
    lat_forward(1, 1)

    quarter = 2 * z_lo + core
    kind_even = jnp.where(j == 1, 0, jnp.where(j == 2, 2, 1))
    kind_odd = jnp.where(j < 2, 2, 0)
    kind_mine = jnp.where(x_odd, kind_odd, kind_even)
    kind_theirs = jnp.where(x_odd, kind_even, kind_odd)
    target = jnp.where(x_odd, lax.rem(j + 2, 4), j + 1 - 2 * lax.rem(j, 2))
    w_slot = lax.rem(target + j, 4)
    w_kind = (3 * j + w_slot) // 4

    def w_rows(kind, q):
        return wq.at[kind, pl.ds(pl.multiple_of(q * QUARTER, 16), QUARTER)]

    send(
        qw_hbm.at[pl.ds(pl.multiple_of(w_slot * COLS + quarter * QUARTER, 16), QUARTER)],
        w_rows(w_kind, quarter), w_r.at[0], (b, p, target),
    )
    for k in (1, 3, 2):
        send(kvs.at[px_peer[k]], kvg.at[0, j], kv_r.at[0, j], px_id[k])

    for i in range(1, 8):
        received(st_py.at[i], sp_r.at[i])
    mean, squares = merge(
        [st_py[i, 0:8] for i in range(8)], [st_py[i, 8:16] for i in range(8)], float(ENTRIES)
    )
    st_mid[0:8] = mean
    st_mid[8:16] = squares
    st_px[j] = st_mid[...]
    for k in range(1, 4):
        send(st_mid, st_px.at[j], sx_r.at[j], px_id[k])
    kv_second(0)
    for k in range(1, 4):
        received(st_px.at[px_peer[k]], sx_r.at[px_peer[k]])
    mean, squares = merge(
        [st_px[i, 0:8] for i in range(4)], [st_px[i, 8:16] for i in range(4)], float(ENTRIES * 8)
    )
    spread_all = squares * (1.0 / (ENTRIES * 32))
    gn_mean = to_channels(mean)
    gn_scale = to_channels(lax.rsqrt(spread_all + 1e-06)) * gng_ref[...].reshape(1, WIDTH)
    gn_shift = gnb_ref[...].reshape(1, WIDTH)

    def own_columns(ref):
        row = ref[...].reshape(1, WIDTH)
        out = row[:, 0:COLS]
        for t in range(1, N_PX):
            out = jnp.where(j == t, row[:, t * COLS : (t + 1) * COLS], out)
        return out

    proj_bias = own_columns(pb_ref)
    ln_gain = own_columns(lng_ref)
    ln_bias = own_columns(lnb_ref)
    lane8 = lax.broadcasted_iota(jnp.int32, (TOK, 8), 1)
    row8 = lax.broadcasted_iota(jnp.int32, (8, TOK), 0)

    def project(t, source):
        grouped = ((source[...].astype(F32) - gn_mean) * gn_scale + gn_shift).astype(BF16)
        out = mm_t(grouped, pw_ref[...]) + proj_bias
        proj[t] = out
        part_mean = jnp.sum(out, axis=1, keepdims=True) * (1.0 / COLS)
        off = out - part_mean
        part_squares = jnp.sum(off * off, axis=1, keepdims=True)
        ln_out[t] = jnp.where(lane8 < 4, part_mean, part_squares).T

    loads[3].wait()
    project(j, lat_ref)
    received(w_rows(kind_mine, quarter), w_r.at[0])
    send(w_rows(kind_mine, quarter), w_rows(kind_mine, quarter), w_r.at[1], x_pair_id)
    for k, half in ((3, 1), (1, 0)):
        lat_received(k, half)
        project(px_peer[k], latg.at[px_peer[k]])
    kv_opposite(0, 0)
    lat_received(2, 0)
    lat_received(2, 1)
    project(px_peer[2], latg.at[px_peer[2]])

    for k in range(1, 4):
        send(ln_out, ln_in.at[j], ln_r.at[j], px_id[k])
    ln_in[j] = ln_out[...]
    for k in (1, 3, 2):
        kv_received(0, k)
        kv_first(k)
    received(w_rows(kind_theirs, quarter), w_r.at[1])
    for i, kind in enumerate((kind_mine, kind_theirs)):
        send(w_rows(kind, quarter), w_rows(kind, quarter), w_r.at[2 + i], across_id)
    for i, kind in enumerate((kind_mine, kind_theirs)):
        send(w_rows(kind, quarter), w_rows(kind, quarter), w_r.at[4 + i], core_id)

    for k in range(1, 4):
        received(ln_in.at[px_peer[k]], ln_r.at[px_peer[k]])
    tails = []
    for t in range(N_PX):
        mean, squares = merge(
            [ln_in[d, t, 0:1] for d in range(N_PX)], [ln_in[d, t, 4:5] for d in range(N_PX)], float(COLS)
        )
        scale = lax.rsqrt(squares * (1.0 / WIDTH) + 1e-05)
        both = jnp.where(row8 < 4, jnp.broadcast_to(mean, (8, TOK)), jnp.broadcast_to(scale, (8, TOK)))
        both = both.T
        normed = ((proj[t] - both[:, 0:1]) * both[:, 4:5] * ln_gain + ln_bias).astype(BF16)
        body = jnp.where(even, normed[:, 0:256], normed[:, HEAD_DIM:])
        tails.append(jnp.where(even, normed[:, 256:], normed[:, 0:HEAD_DIM]))
        for i in range(2):
            start = i * 256 + (t % 2) * TOK
            nrm[j, t // 2, start : start + TOK] = body[:, i * 128 : (i + 1) * 128]
    for half in range(2):
        nrm[j, half, 512:] = jnp.concatenate(tails[2 * half : 2 * half + 2], axis=1)
    for half in range(2):
        for k, own_half in ((1, half), (3, 1 - half)):
            send(nrm.at[j, own_half], nrm.at[j, own_half], nrm_r.at[j, own_half], px_id[k])

    def nrm_received(k, half):
        t = px_peer[k]
        received(nrm.at[t, half], nrm_r.at[t, half])

    def nrm_forward(k, half):
        t = px_peer[k]
        nrm_received(k, half)
        send(nrm.at[t, half], nrm.at[t, half], nrm_r.at[t, half], px_id[4 - k])

    kv_opposite(0, 1)
    nrm_forward(3, 0)
    nrm_forward(1, 1)
    kv_second(1)
    kv_opposite(1, 0)

    across_q = 2 * (1 - z_lo) + core
    for i, kind in enumerate((kind_mine, kind_theirs)):
        received(w_rows(kind, across_q), w_r.at[2 + i])
        send(w_rows(kind, across_q), w_rows(kind, across_q), w_r.at[6 + i], core_id)
    for k in (3, 2):
        kv_opposite(0, k)
    for k in (3, 2):
        for dx in (1, 3):
            kv_across(dx, k)
    for i, kind in enumerate((kind_mine, kind_theirs)):
        received(w_rows(kind, 2 * z_lo + 1 - core), w_r.at[4 + i])
        received(w_rows(kind, 2 * (1 - z_lo) + 1 - core), w_r.at[6 + i])
    loads[4].wait()

    def weight_lanes(start, size):
        return wq[:, :, pl.ds(start, size)].reshape(3 * COLS, size)

    def part(d):
        start = pl.multiple_of((d // 2) * 640 + lax.rem(d, 2) * 384, 128)
        rows = jnp.concatenate(
            [jnp.concatenate([nrm[d, half, 0:256], nrm[d, half, 256:512]], axis=1) for half in range(2)], axis=0
        )
        return mm_t(rows, weight_lanes(start, 256))

    qkv_acc[...] = part(j)
    nrm_received(3, 1)
    qkv_acc[...] += part(px_peer[3])
    nrm_received(1, 0)
    qkv_acc[...] += part(px_peer[1])
    nrm_received(2, 0)
    nrm_received(2, 1)
    qkv_acc[...] += part(px_peer[2])
    tail = jnp.concatenate(
        [
            jnp.concatenate([nrm[d, t // 2, 512:, (t % 2) * 64 : (t % 2) * 64 + 64] for d in range(N_PX)], axis=1)
            for t in range(N_PX)
        ],
        axis=0,
    )
    tail_weight = jnp.concatenate([weight_lanes(256, 128), weight_lanes(896, 128)], axis=1)
    qkv_acc[...] += mm_t(tail, tail_weight)
    blank = jnp.zeros((TOK, HEAD_DIM), BF16)
    for t in range(N_PX):
        rows = qkv_acc[t * TOK : (t + 1) * TOK, :]
        query = (rows[:, 0:COLS] * HEAD_DIM ** (-0.5)).astype(BF16)
        key = rows[:, COLS : 2 * COLS].astype(BF16)
        value = rows[:, 2 * COLS :].astype(BF16)
        for h in range(GROUP_HEADS):
            lanes = slice(h * HEAD_DIM, (h + 1) * HEAD_DIM)
            q_buf[t, :, h * 128 : (h + 1) * 128] = jnp.concatenate([query[:, lanes], blank], axis=1)
            fkv[t, :, h * 128 : (h + 1) * 128] = jnp.concatenate([key[:, lanes], value[:, lanes]], axis=1)
    for k in range(1, 4):
        send(fkv.at[px_peer[k]], fresh_out.at[j], fr_r.at[j], px_id[k])
    keep_fresh = pltpu.make_async_copy(fkv.at[j], fresh_out.at[j], load_s.at[5])
    keep_fresh.start()

    for i in range(1, 4):
        for k in range(N_PX):
            kv_received(i, k)
    kv_opposite(1, 1)
    for k in (3, 2):
        kv_across(2, k)
    lane = lax.broadcasted_iota(jnp.int32, (2048, 128), 1)

    def head_lanes(h):
        return slice(h * 128, (h + 1) * 128)

    def first_keys(h, t):
        lanes = head_lanes(h)
        parts = [fkv[t, :, lanes] if u == t else kvg[0, u, :, lanes] for u in range(N_PX)]
        parts.append(kvg[1:4, :, :, lanes].reshape(1536, 128))
        return jnp.concatenate(parts, axis=0)

    def second_keys(h, t):
        return kvg[4:8, :, :, head_lanes(h)].reshape(2048, 128)

    def weigh(weight, keys):
        return mm(weight.astype(BF16), jnp.where(lane < HEAD_DIM, jnp.ones((), BF16), keys))

    items = [(h, t) for t in range(N_PX) for h in range(GROUP_HEADS)]
    score = mm_t(q_buf[items[0][1], :, head_lanes(items[0][0])], first_keys(*items[0]))
    for n, (h, t) in enumerate(items):
        following = None
        if n + 1 < len(items):
            h2, t2 = items[n + 1]
            following = mm_t(q_buf[t2, :, head_lanes(h2)], first_keys(h2, t2))
        new = jnp.max(score, axis=1, keepdims=True)
        weight = jnp.exp(score - new)
        top[h, t] = jnp.broadcast_to(new, (TOK, 128))
        acc[h, t] = weigh(weight, first_keys(h, t))
        score = following

    for i in range(4, 8):
        for k in range(N_PX):
            kv_received(i, k)
    order = [px_peer[1], px_peer[2], px_peer[3], j]
    items = [(h, k) for k in range(N_PX) for h in range(GROUP_HEADS)]
    score = mm_t(q_buf[order[0], :, head_lanes(0)], second_keys(0, 0))
    outs = []
    for n, (h, k) in enumerate(items):
        following = None
        if n + 1 < len(items):
            h2, k2 = items[n + 1]
            following = mm_t(q_buf[order[k2], :, head_lanes(h2)], second_keys(h2, k2))
        t = order[k]
        old = top[h, t]
        new = jnp.maximum(old, jnp.max(score, axis=1, keepdims=True))
        weight = jnp.exp(score - new[:, 0:1])
        total = acc[h, t] * jnp.exp(old - new) + weigh(weight, second_keys(h, k))
        outs.append(total[:, HEAD_DIM:] / total[:, 0:HEAD_DIM])
        if h == GROUP_HEADS - 1:
            outs.append(jnp.zeros((TOK, HEAD_DIM), F32))
            ost[k] = jnp.concatenate(outs, axis=1).astype(BF16)
            outs = []
            if k < 3:
                send(ost.at[k], att_out.at[j], or_r.at[j], px_id[k + 1])
        score = following

    keep_att = pltpu.make_async_copy(ost.at[3], att_out.at[j], load_s.at[6])
    keep_att.start()
    for k in range(1, 4):
        received(fresh_out.at[px_peer[k]], fr_r.at[px_peer[k]])
    for k in range(1, 4):
        received(att_out.at[px_peer[k]], or_r.at[px_peer[k]])
    keep_fresh.wait()
    keep_att.wait()
    for copy in sends:
        copy.wait_send()


def lay_out(fresh_ref, att_in_ref, att_ref, fk_ref, fv_ref):
    for first, out_ref in ((0, fk_ref), (HEAD_DIM, fv_ref)):
        out_ref[...] = jnp.concatenate(
            [
                fresh_ref[g, :, h * 128 + first : h * 128 + first + HEAD_DIM]
                for g in range(N_PX)
                for h in range(GROUP_HEADS)
            ],
            axis=1,
        )
    att_ref[...] = jnp.concatenate([att_in_ref[g, :, 0:COLS] for g in range(N_PX)], axis=1)


def shards(
    latents, gn_gain, gn_bias, proj_weight, proj_bias, ln_gain, ln_bias, qkv_weight, stale_keys, stale_values
):
    patch_rows, patch_cols, width = latents.shape
    tokens = patch_rows * patch_cols
    dma = pltpu.SemaphoreType.DMA
    vmem = pl.BlockSpec(memory_space=pltpu.VMEM)
    hbm = pl.BlockSpec(memory_space=pl.ANY)
    out = jax.ShapeDtypeStruct((tokens, width), BF16)
    scratch = [
        pltpu.VMEM((TOK, WIDTH), BF16),
        pltpu.VMEM((TOK, WIDTH), BF16),
        pltpu.VMEM((TOK, WIDTH), BF16),
        pltpu.VMEM((COLS, WIDTH), BF16),
        pltpu.VMEM((N_PX, TOK, WIDTH), BF16),
        pltpu.VMEM((16, 128), F32),
        pltpu.VMEM((N_PY, 16, 128), F32),
        pltpu.VMEM((16, 128), F32),
        pltpu.VMEM((N_PX, 16, 128), F32),
        pltpu.VMEM((N_PX, TOK, COLS), F32),
        pltpu.VMEM((N_PX, 8, TOK), F32),
        pltpu.VMEM((N_PX, N_PX, 8, TOK), F32),
        pltpu.VMEM((N_PX, 2, 640, 128), BF16),
        pltpu.VMEM((3, COLS, WIDTH), BF16),
        pltpu.VMEM((4 * TOK, 3 * COLS), F32),
        pltpu.VMEM((N_PX, TOK, PAIR), BF16),
        pltpu.VMEM((N_PX, TOK, PAIR), BF16),
        pltpu.VMEM((N_PX, TOK, PAIR), BF16),
        pltpu.VMEM((N_PY, N_PX, TOK, PAIR), BF16),
        pltpu.VMEM((GROUP_HEADS, N_PX, TOK, 128), F32),
        pltpu.VMEM((GROUP_HEADS, N_PX, TOK, 128), F32),
        pltpu.VMEM((N_PX, TOK, 384), BF16),
    ]
    sems = [(7,), (80,), (4, 2), (8,), (4,), (4,), (4, 2), (8,), (8, 4), (4,), (4,)]
    fresh, groups = pl.pallas_call(
        kernel,
        out_shape=(
            jax.ShapeDtypeStruct((N_PX, TOK, PAIR), BF16),
            jax.ShapeDtypeStruct((N_PX, TOK, 384), BF16),
        ),
        in_specs=[hbm, vmem, vmem, hbm, vmem, vmem, vmem, hbm, hbm, hbm],
        out_specs=(hbm, hbm),
        scratch_shapes=scratch + [dma(shape) for shape in sems],
        compiler_params=pltpu.CompilerParams(
            collective_id=0, has_side_effects=True, vmem_limit_bytes=56 * 1024 * 1024
        ),
        name="patch_attention",
    )(
        latents.reshape(tokens, width),
        gn_gain, gn_bias, proj_weight.T, proj_bias, ln_gain, ln_bias, qkv_weight.T,
        stale_keys.reshape(tokens, width), stale_values.reshape(tokens, width),
    )
    attended, fresh_keys, fresh_values = pl.pallas_call(
        lay_out,
        out_shape=(out, out, out),
        in_specs=[vmem, vmem],
        out_specs=(vmem, vmem, vmem),
        name="lay_out",
    )(fresh, groups)
    shape = (patch_rows, patch_cols, width)
    return attended.reshape(shape), fresh_keys.reshape(shape), fresh_values.reshape(shape)


def solution(mesh):
    split = P(("batch", "py"), "px", None)
    return jax.shard_map(
        shards,
        mesh=mesh,
        in_specs=(split, P(), P(), P(None, "px"), P(), P(), P(), P(None, "px"), split, split),
        out_specs=(split, split, split),
        check_vma=False,
    )
```

```python
import jax
import jax.numpy as jnp
from jax import lax
from jax.experimental import pallas as pl
from jax.experimental.pallas import tpu as pltpu
from jax.sharding import PartitionSpec as P

MESH = pl.DeviceIdType.MESH
HIGHEST = lax.Precision.HIGHEST
BF16 = jnp.bfloat16
F32 = jnp.float32

WIDTH = 1280
HEADS = 20
HEAD_DIM = 64
GROUPS = 32
N_PY = 8
N_PX = 4
TOK = 128
GROUP_HEADS = HEADS // N_PX
COLS = WIDTH // N_PX
QUARTER = COLS // 4
PAIR = GROUP_HEADS * 2 * HEAD_DIM
ENTRIES = TOK * (WIDTH // GROUPS)

SLOTS = ((0, 0), (0, 1), (1, 0), (3, 0), (1, 1), (3, 1), (2, 0), (2, 1))


def slot_of(dx, dz):
    return SLOTS.index((dx % 4, dz))


def mm(a, b, precision=None):
    return lax.dot_general(
        a, b, (((1,), (0,)), ((), ())), precision=precision, preferred_element_type=F32
    )


def mm_t(a, b, precision=None):
    return lax.dot_general(
        a, b, (((1,), (1,)), ((), ())), precision=precision, preferred_element_type=F32
    )


def merge(means, squares, count):
    n = len(means)
    mean = sum(means[1:], means[0]) * (1.0 / n)
    total = sum(squares[1:], squares[0])
    for part in means:
        total = total + count * (part - mean) * (part - mean)
    return mean, total


def kernel(
    lat_hbm, gng_ref, gnb_ref, pw_hbm, pb_ref, lng_ref, lnb_ref, qw_hbm, sk_hbm, sv_hbm,
    fresh_out, att_out,
    lat_ref, sk_ref, sv_ref, pw_ref, latg, st_out, st_py, st_mid, st_px, proj, ln_out, ln_in, nrm,
    wq, qkv_acc, q_buf, fkv, kvs, kvg, acc, top, ost,
    load_s, send_s, lat_r, sp_r, sx_r, ln_r, nrm_r, w_r, kv_r, fr_r, or_r,
):
    b = lax.axis_index("batch")
    p = lax.axis_index("py")
    j = lax.axis_index("px")
    core = lax.rem(b, 2)
    x, z_lo = p // 2, lax.rem(p, 2)
    x_odd = lax.rem(x, 2) == 1
    even = lax.rem(j, 2) == 0

    px_peer = [(j + k) % N_PX for k in range(N_PX)]
    px_id = [(b, p, t) for t in px_peer]
    py_id = [(b, lax.rem(x + dx, 4) * 2 + (z_lo if dz == 0 else 1 - z_lo), j) for dx, dz in SLOTS]
    core_id = (b + 1 - 2 * core, p, j)
    across_id = (lax.rem(b + jnp.where(z_lo == 1, 2, 6), 8), p + 1 - 2 * z_lo, j)
    x_pair_id = (b, p + 2 - 4 * lax.rem(x, 2), j)

    own_slot = jnp.where(even, 0, 2)
    kind_own = jnp.where(j == 0, 0, jnp.where(j == 3, 2, 1))
    loads = [
        pltpu.make_async_copy(src, dst, load_s.at[i])
        for i, (src, dst) in enumerate(
            (
                (sk_hbm, sk_ref), (sv_hbm, sv_ref), (lat_hbm, lat_ref), (pw_hbm, pw_ref),
                (qw_hbm.at[pl.ds(pl.multiple_of(own_slot * COLS, 16), COLS)], wq.at[kind_own]),
            )
        )
    ]
    for load in loads:
        load.start()

    barrier = pltpu.get_barrier_semaphore()
    peers = px_id[1:] + py_id[1:] + [core_id, across_id]
    for peer in peers:
        pl.semaphore_signal(barrier, inc=1, device_id=peer, device_id_type=MESH)

    loads[0].wait()
    loads[1].wait()
    for t in range(N_PX):
        for h in range(GROUP_HEADS):
            lanes = slice((t * GROUP_HEADS + h) * HEAD_DIM, (t * GROUP_HEADS + h + 1) * HEAD_DIM)
            kvs[t, :, h * 128 : (h + 1) * 128] = jnp.concatenate(
                [sk_ref[:, lanes], sv_ref[:, lanes]], axis=1
            )
    kvg[0, j] = kvs[j]

    pl.semaphore_wait(barrier, len(peers))

    sends = []

    def send(src, dst, r_sem, peer):
        copy = pltpu.make_async_remote_copy(
            src_ref=src, dst_ref=dst, send_sem=send_s.at[len(sends)], recv_sem=r_sem,
            device_id=peer, device_id_type=MESH,
        )
        copy.start()
        sends.append(copy)

    def received(dst, r_sem):
        pltpu.make_async_remote_copy(
            src_ref=dst, dst_ref=dst, send_sem=send_s.at[0], recv_sem=r_sem,
            device_id=px_id[1], device_id_type=MESH,
        ).wait_recv()

    halves = (pl.ds(0, TOK // 2), pl.ds(TOK // 2, TOK // 2))

    kv_done = set()

    def kv_received(slot, k):
        if (slot, k) not in kv_done:
            kv_done.add((slot, k))
            received(kvg.at[slot, px_peer[k]], kv_r.at[slot, px_peer[k]])

    def kv_send(slot, k, to_slot, peer):
        u = px_peer[k]
        send(kvg.at[slot, u], kvg.at[to_slot, u], kv_r.at[to_slot, u], peer)

    def kv_sides(z, k):
        for dx in (1, 3):
            kv_send(z, k, slot_of(-dx, z), py_id[slot_of(dx, 0)])

    def kv_first(k):
        kv_send(0, k, 1, py_id[1])
        kv_sides(0, k)

    def kv_opposite(z, k):
        dx = 3 if k % 2 == 0 else 1
        kv_received(slot_of(dx, z), k)
        kv_send(slot_of(dx, z), k, slot_of(2, z), py_id[slot_of(-dx, 0)])

    def kv_second(k):
        kv_received(1, k)
        kv_sides(1, k)

    def kv_across(dx, k):
        kv_received(slot_of(dx, 0), k)
        kv_send(slot_of(dx, 0), k, slot_of(dx, 1), py_id[1])

    for k in (1, 3, 2):
        send(kvs.at[px_peer[k]], kvg.at[0, j], kv_r.at[0, j], px_id[k])
    kv_first(0)

    for half in range(2):
        for k, own_half in ((1, half), (3, 1 - half)):
            rows = halves[own_half]
            send(lat_hbm.at[rows], latg.at[j, rows], lat_r.at[j, own_half], px_id[k])

    def lat_received(k, half):
        t = px_peer[k]
        received(latg.at[t, halves[half]], lat_r.at[t, half])

    def lat_forward(k, half):
        t = px_peer[k]
        lat_received(k, half)
        rows = halves[half]
        send(latg.at[t, rows], latg.at[t, rows], lat_r.at[t, half], px_id[4 - k])

    chan = lax.broadcasted_iota(jnp.int32, (WIDTH, 128), 0)
    group = lax.broadcasted_iota(jnp.int32, (WIDTH, 128), 1) * (WIDTH // GROUPS)
    member = jnp.where((chan >= group) & (chan < group + WIDTH // GROUPS), 1.0, 0.0).astype(F32)

    def to_groups(row):
        return mm(jnp.broadcast_to(row, (8, WIDTH)), member, HIGHEST)

    def to_channels(row):
        return mm_t(row, member, HIGHEST)[0:1]

    loads[2].wait()
    own = lat_ref[...].astype(F32)
    own_mean = to_groups(jnp.sum(own, axis=0, keepdims=True)) * (1.0 / ENTRIES)
    centered = own - to_channels(own_mean)
    own_squares = to_groups(jnp.sum(centered * centered, axis=0, keepdims=True))
    st_out[0:8] = own_mean
    st_out[8:16] = own_squares
    st_py[0] = st_out[...]
    for i in range(1, 8):
        dx, dz = SLOTS[i]
        send(st_out, st_py.at[slot_of(-dx, dz)], sp_r.at[slot_of(-dx, dz)], py_id[i])


    quarter = 2 * z_lo + core
    kind_even = jnp.where(j == 1, 0, jnp.where(j == 2, 2, 1))
    kind_odd = jnp.where(j < 2, 2, 0)
    kind_mine = jnp.where(x_odd, kind_odd, kind_even)
    kind_theirs = jnp.where(x_odd, kind_even, kind_odd)
    target = jnp.where(x_odd, lax.rem(j + 2, 4), j + 1 - 2 * lax.rem(j, 2))
    w_slot = lax.rem(target + j, 4)
    w_kind = (3 * j + w_slot) // 4

    def w_rows(kind, q):
        return wq.at[kind, pl.ds(pl.multiple_of(q * QUARTER, 16), QUARTER)]

    for i in range(1, 8):
        received(st_py.at[i], sp_r.at[i])
    mean, squares = merge(
        [st_py[i, 0:8] for i in range(8)], [st_py[i, 8:16] for i in range(8)], float(ENTRIES)
    )
    st_mid[0:8] = mean
    st_mid[8:16] = squares
    st_px[j] = st_mid[...]
    for k in range(1, 4):
        send(st_mid, st_px.at[j], sx_r.at[j], px_id[k])
    kv_second(0)
    kv_opposite(0, 0)
    lat_forward(3, 0)
    lat_forward(1, 1)
    send(
        qw_hbm.at[pl.ds(pl.multiple_of(w_slot * COLS + quarter * QUARTER, 16), QUARTER)],
        w_rows(w_kind, quarter), w_r.at[0], (b, p, target),
    )
    for k in (1, 3, 2):
        kv_received(0, k)
        kv_first(k)
    for k in range(1, 4):
        received(st_px.at[px_peer[k]], sx_r.at[px_peer[k]])
    mean, squares = merge(
        [st_px[i, 0:8] for i in range(4)], [st_px[i, 8:16] for i in range(4)], float(ENTRIES * 8)
    )
    spread_all = squares * (1.0 / (ENTRIES * 32))
    gn_mean = to_channels(mean)
    gn_scale = to_channels(lax.rsqrt(spread_all + 1e-06)) * gng_ref[...].reshape(1, WIDTH)
    gn_shift = gnb_ref[...].reshape(1, WIDTH)

    def own_columns(ref):
        row = ref[...].reshape(1, WIDTH)
        out = row[:, 0:COLS]
        for t in range(1, N_PX):
            out = jnp.where(j == t, row[:, t * COLS : (t + 1) * COLS], out)
        return out

    proj_bias = own_columns(pb_ref)
    ln_gain = own_columns(lng_ref)
    ln_bias = own_columns(lnb_ref)
    lane8 = lax.broadcasted_iota(jnp.int32, (TOK, 8), 1)
    row8 = lax.broadcasted_iota(jnp.int32, (8, TOK), 0)

    def project(t, source):
        grouped = ((source[...].astype(F32) - gn_mean) * gn_scale + gn_shift).astype(BF16)
        out = mm_t(grouped, pw_ref[...]) + proj_bias
        proj[t] = out
        part_mean = jnp.sum(out, axis=1, keepdims=True) * (1.0 / COLS)
        off = out - part_mean
        part_squares = jnp.sum(off * off, axis=1, keepdims=True)
        ln_out[t] = jnp.where(lane8 < 4, part_mean, part_squares).T

    loads[3].wait()
    project(j, lat_ref)
    for k, half in ((3, 1), (1, 0)):
        lat_received(k, half)
        project(px_peer[k], latg.at[px_peer[k]])
    kv_second(1)
    lat_received(2, 0)
    lat_received(2, 1)
    project(px_peer[2], latg.at[px_peer[2]])

    for k in range(1, 4):
        send(ln_out, ln_in.at[j], ln_r.at[j], px_id[k])
    ln_in[j] = ln_out[...]
    received(w_rows(kind_mine, quarter), w_r.at[0])
    send(w_rows(kind_mine, quarter), w_rows(kind_mine, quarter), w_r.at[1], x_pair_id)
    for z, k in ((0, 1), (1, 0), (0, 3)):
        kv_opposite(z, k)
    for k in range(1, 4):
        received(ln_in.at[px_peer[k]], ln_r.at[px_peer[k]])
    tails = []
    for t in range(N_PX):
        mean, squares = merge(
            [ln_in[d, t, 0:1] for d in range(N_PX)], [ln_in[d, t, 4:5] for d in range(N_PX)], float(COLS)
        )
        scale = lax.rsqrt(squares * (1.0 / WIDTH) + 1e-05)
        both = jnp.where(row8 < 4, jnp.broadcast_to(mean, (8, TOK)), jnp.broadcast_to(scale, (8, TOK)))
        both = both.T
        normed = ((proj[t] - both[:, 0:1]) * both[:, 4:5] * ln_gain + ln_bias).astype(BF16)
        body = jnp.where(even, normed[:, 0:256], normed[:, HEAD_DIM:])
        tails.append(jnp.where(even, normed[:, 256:], normed[:, 0:HEAD_DIM]))
        for i in range(2):
            start = i * 256 + (t % 2) * TOK
            nrm[j, t // 2, start : start + TOK] = body[:, i * 128 : (i + 1) * 128]
    for half in range(2):
        nrm[j, half, 512:] = jnp.concatenate(tails[2 * half : 2 * half + 2], axis=1)
    for half in range(2):
        for k, own_half in ((1, half), (3, 1 - half)):
            send(nrm.at[j, own_half], nrm.at[j, own_half], nrm_r.at[j, own_half], px_id[k])

    def nrm_received(k, half):
        t = px_peer[k]
        received(nrm.at[t, half], nrm_r.at[t, half])

    def nrm_forward(k, half):
        t = px_peer[k]
        nrm_received(k, half)
        send(nrm.at[t, half], nrm.at[t, half], nrm_r.at[t, half], px_id[4 - k])

    received(w_rows(kind_theirs, quarter), w_r.at[1])
    for i, kind in enumerate((kind_mine, kind_theirs)):
        send(w_rows(kind, quarter), w_rows(kind, quarter), w_r.at[2 + i], across_id)
    for i, kind in enumerate((kind_mine, kind_theirs)):
        send(w_rows(kind, quarter), w_rows(kind, quarter), w_r.at[4 + i], core_id)
    for dx in (1, 3):
        kv_across(dx, 3)
    kv_opposite(0, 2)
    nrm_forward(3, 0)
    nrm_forward(1, 1)
    kv_opposite(1, 1)

    across_q = 2 * (1 - z_lo) + core
    for i, kind in enumerate((kind_mine, kind_theirs)):
        received(w_rows(kind, across_q), w_r.at[2 + i])
        send(w_rows(kind, across_q), w_rows(kind, across_q), w_r.at[6 + i], core_id)
    for dx in (1, 3):
        kv_across(dx, 2)
    for i, kind in enumerate((kind_mine, kind_theirs)):
        received(w_rows(kind, 2 * z_lo + 1 - core), w_r.at[4 + i])
        received(w_rows(kind, 2 * (1 - z_lo) + 1 - core), w_r.at[6 + i])
    loads[4].wait()

    def weight_lanes(start, size):
        return wq[:, :, pl.ds(start, size)].reshape(3 * COLS, size)

    def part(d):
        start = pl.multiple_of((d // 2) * 640 + lax.rem(d, 2) * 384, 128)
        rows = jnp.concatenate(
            [jnp.concatenate([nrm[d, half, 0:256], nrm[d, half, 256:512]], axis=1) for half in range(2)], axis=0
        )
        return mm_t(rows, weight_lanes(start, 256))

    qkv_acc[...] = part(j)
    nrm_received(3, 1)
    qkv_acc[...] += part(px_peer[3])
    nrm_received(1, 0)
    qkv_acc[...] += part(px_peer[1])
    kv_across(2, 3)
    nrm_received(2, 0)
    nrm_received(2, 1)
    qkv_acc[...] += part(px_peer[2])
    tail = jnp.concatenate(
        [
            jnp.concatenate([nrm[d, t // 2, 512:, (t % 2) * 64 : (t % 2) * 64 + 64] for d in range(N_PX)], axis=1)
            for t in range(N_PX)
        ],
        axis=0,
    )
    tail_weight = jnp.concatenate([weight_lanes(256, 128), weight_lanes(896, 128)], axis=1)
    qkv_acc[...] += mm_t(tail, tail_weight)
    blank = jnp.zeros((TOK, HEAD_DIM), BF16)
    for t in range(N_PX):
        rows = qkv_acc[t * TOK : (t + 1) * TOK, :]
        query = (rows[:, 0:COLS] * HEAD_DIM ** (-0.5)).astype(BF16)
        key = rows[:, COLS : 2 * COLS].astype(BF16)
        value = rows[:, 2 * COLS :].astype(BF16)
        for h in range(GROUP_HEADS):
            lanes = slice(h * HEAD_DIM, (h + 1) * HEAD_DIM)
            q_buf[t, :, h * 128 : (h + 1) * 128] = jnp.concatenate([query[:, lanes], blank], axis=1)
            fkv[t, :, h * 128 : (h + 1) * 128] = jnp.concatenate([key[:, lanes], value[:, lanes]], axis=1)
    for k in range(1, 4):
        send(fkv.at[px_peer[k]], fresh_out.at[j], fr_r.at[j], px_id[k])
    keep_fresh = pltpu.make_async_copy(fkv.at[j], fresh_out.at[j], load_s.at[5])
    keep_fresh.start()

    kv_across(2, 2)
    for i in range(1, 4):
        for k in range(N_PX):
            kv_received(i, k)
    lane = lax.broadcasted_iota(jnp.int32, (2048, 128), 1)

    def head_lanes(h):
        return slice(h * 128, (h + 1) * 128)

    def first_keys(h, t):
        lanes = head_lanes(h)
        parts = [fkv[t, :, lanes] if u == t else kvg[0, u, :, lanes] for u in range(N_PX)]
        parts.append(kvg[1:4, :, :, lanes].reshape(1536, 128))
        return jnp.concatenate(parts, axis=0)

    def second_keys(h, t):
        return kvg[4:8, :, :, head_lanes(h)].reshape(2048, 128)

    def weigh(weight, keys):
        return mm(weight.astype(BF16), jnp.where(lane < HEAD_DIM, jnp.ones((), BF16), keys))

    items = [(h, t) for t in range(N_PX) for h in range(GROUP_HEADS)]
    score = mm_t(q_buf[items[0][1], :, head_lanes(items[0][0])], first_keys(*items[0]))
    for n, (h, t) in enumerate(items):
        following = None
        if n + 1 < len(items):
            h2, t2 = items[n + 1]
            following = mm_t(q_buf[t2, :, head_lanes(h2)], first_keys(h2, t2))
        new = jnp.max(score, axis=1, keepdims=True)
        weight = jnp.exp(score - new)
        top[h, t] = jnp.broadcast_to(new, (TOK, 128))
        acc[h, t] = weigh(weight, first_keys(h, t))
        score = following

    for i in range(4, 8):
        for k in range(N_PX):
            kv_received(i, k)
    order = [px_peer[1], px_peer[2], px_peer[3], j]
    items = [(h, k) for k in range(N_PX) for h in range(GROUP_HEADS)]
    score = mm_t(q_buf[order[0], :, head_lanes(0)], second_keys(0, 0))
    outs = []
    for n, (h, k) in enumerate(items):
        following = None
        if n + 1 < len(items):
            h2, k2 = items[n + 1]
            following = mm_t(q_buf[order[k2], :, head_lanes(h2)], second_keys(h2, k2))
        t = order[k]
        old = top[h, t]
        new = jnp.maximum(old, jnp.max(score, axis=1, keepdims=True))
        weight = jnp.exp(score - new[:, 0:1])
        total = acc[h, t] * jnp.exp(old - new) + weigh(weight, second_keys(h, k))
        outs.append(total[:, HEAD_DIM:] / total[:, 0:HEAD_DIM])
        if h == GROUP_HEADS - 1:
            outs.append(jnp.zeros((TOK, HEAD_DIM), F32))
            ost[k] = jnp.concatenate(outs, axis=1).astype(BF16)
            outs = []
            if k < 3:
                send(ost.at[k], att_out.at[j], or_r.at[j], px_id[k + 1])
        score = following

    keep_att = pltpu.make_async_copy(ost.at[3], att_out.at[j], load_s.at[6])
    keep_att.start()
    for k in range(1, 4):
        received(fresh_out.at[px_peer[k]], fr_r.at[px_peer[k]])
    for k in range(1, 4):
        received(att_out.at[px_peer[k]], or_r.at[px_peer[k]])
    keep_fresh.wait()
    keep_att.wait()
    for copy in sends:
        copy.wait_send()


def lay_out(fresh_ref, att_in_ref, att_ref, fk_ref, fv_ref):
    for first, out_ref in ((0, fk_ref), (HEAD_DIM, fv_ref)):
        out_ref[...] = jnp.concatenate(
            [
                fresh_ref[g, :, h * 128 + first : h * 128 + first + HEAD_DIM]
                for g in range(N_PX)
                for h in range(GROUP_HEADS)
            ],
            axis=1,
        )
    att_ref[...] = jnp.concatenate([att_in_ref[g, :, 0:COLS] for g in range(N_PX)], axis=1)


def shards(
    latents, gn_gain, gn_bias, proj_weight, proj_bias, ln_gain, ln_bias, qkv_weight, stale_keys, stale_values
):
    patch_rows, patch_cols, width = latents.shape
    tokens = patch_rows * patch_cols
    dma = pltpu.SemaphoreType.DMA
    vmem = pl.BlockSpec(memory_space=pltpu.VMEM)
    hbm = pl.BlockSpec(memory_space=pl.ANY)
    out = jax.ShapeDtypeStruct((tokens, width), BF16)
    scratch = [
        pltpu.VMEM((TOK, WIDTH), BF16),
        pltpu.VMEM((TOK, WIDTH), BF16),
        pltpu.VMEM((TOK, WIDTH), BF16),
        pltpu.VMEM((COLS, WIDTH), BF16),
        pltpu.VMEM((N_PX, TOK, WIDTH), BF16),
        pltpu.VMEM((16, 128), F32),
        pltpu.VMEM((N_PY, 16, 128), F32),
        pltpu.VMEM((16, 128), F32),
        pltpu.VMEM((N_PX, 16, 128), F32),
        pltpu.VMEM((N_PX, TOK, COLS), F32),
        pltpu.VMEM((N_PX, 8, TOK), F32),
        pltpu.VMEM((N_PX, N_PX, 8, TOK), F32),
        pltpu.VMEM((N_PX, 2, 640, 128), BF16),
        pltpu.VMEM((3, COLS, WIDTH), BF16),
        pltpu.VMEM((4 * TOK, 3 * COLS), F32),
        pltpu.VMEM((N_PX, TOK, PAIR), BF16),
        pltpu.VMEM((N_PX, TOK, PAIR), BF16),
        pltpu.VMEM((N_PX, TOK, PAIR), BF16),
        pltpu.VMEM((N_PY, N_PX, TOK, PAIR), BF16),
        pltpu.VMEM((GROUP_HEADS, N_PX, TOK, 128), F32),
        pltpu.VMEM((GROUP_HEADS, N_PX, TOK, 128), F32),
        pltpu.VMEM((N_PX, TOK, 384), BF16),
    ]
    sems = [(7,), (80,), (4, 2), (8,), (4,), (4,), (4, 2), (8,), (8, 4), (4,), (4,)]
    fresh, groups = pl.pallas_call(
        kernel,
        out_shape=(
            jax.ShapeDtypeStruct((N_PX, TOK, PAIR), BF16),
            jax.ShapeDtypeStruct((N_PX, TOK, 384), BF16),
        ),
        in_specs=[hbm, vmem, vmem, hbm, vmem, vmem, vmem, hbm, hbm, hbm],
        out_specs=(hbm, hbm),
        scratch_shapes=scratch + [dma(shape) for shape in sems],
        compiler_params=pltpu.CompilerParams(
            collective_id=0, has_side_effects=True, vmem_limit_bytes=56 * 1024 * 1024
        ),
        name="patch_attention",
    )(
        latents.reshape(tokens, width),
        gn_gain, gn_bias, proj_weight.T, proj_bias, ln_gain, ln_bias, qkv_weight.T,
        stale_keys.reshape(tokens, width), stale_values.reshape(tokens, width),
    )
    attended, fresh_keys, fresh_values = pl.pallas_call(
        lay_out,
        out_shape=(out, out, out),
        in_specs=[vmem, vmem],
        out_specs=(vmem, vmem, vmem),
        name="lay_out",
    )(fresh, groups)
    shape = (patch_rows, patch_cols, width)
    return attended.reshape(shape), fresh_keys.reshape(shape), fresh_values.reshape(shape)


def solution(mesh):
    split = P(("batch", "py"), "px", None)
    return jax.shard_map(
        shards,
        mesh=mesh,
        in_specs=(split, P(), P(), P(None, "px"), P(), P(), P(), P(None, "px"), split, split),
        out_specs=(split, split, split),
        check_vma=False,
    )
```

```python
import jax
import jax.numpy as jnp
from jax import lax
from jax.experimental import pallas as pl
from jax.experimental.pallas import tpu as pltpu
from jax.sharding import PartitionSpec as P

MESH = pl.DeviceIdType.MESH
HIGHEST = lax.Precision.HIGHEST
BF16 = jnp.bfloat16
F32 = jnp.float32

WIDTH = 1280
HEADS = 20
HEAD_DIM = 64
GROUPS = 32
N_PY = 8
N_PX = 4
TOK = 128
GROUP_HEADS = HEADS // N_PX
COLS = WIDTH // N_PX
QUARTER = COLS // 4
PAIR = GROUP_HEADS * 2 * HEAD_DIM
ENTRIES = TOK * (WIDTH // GROUPS)

SLOTS = ((0, 0), (0, 1), (1, 0), (3, 0), (1, 1), (3, 1), (2, 0), (2, 1))


def slot_of(dx, dz):
    return SLOTS.index((dx % 4, dz))


def mm(a, b, precision=None):
    return lax.dot_general(
        a, b, (((1,), (0,)), ((), ())), precision=precision, preferred_element_type=F32
    )


def mm_t(a, b, precision=None):
    return lax.dot_general(
        a, b, (((1,), (1,)), ((), ())), precision=precision, preferred_element_type=F32
    )


def merge(means, squares, count):
    n = len(means)
    mean = sum(means[1:], means[0]) * (1.0 / n)
    total = sum(squares[1:], squares[0])
    for part in means:
        total = total + count * (part - mean) * (part - mean)
    return mean, total


def kernel(
    lat_hbm, gng_ref, gnb_ref, pw_hbm, pb_ref, lng_ref, lnb_ref, qw_hbm, sk_hbm, sv_hbm,
    fresh_out, att_out,
    lat_ref, sk_ref, sv_ref, pw_ref, latg, st_out, st_py, st_mid, st_px, proj, ln_out, ln_in, nrm,
    wq, qkv_acc, q_buf, fkv, kvs, kvg, acc, top, ost,
    load_s, send_s, lat_r, sp_r, sx_r, ln_r, nrm_r, w_r, kv_r, fr_r, or_r,
):
    b = lax.axis_index("batch")
    p = lax.axis_index("py")
    j = lax.axis_index("px")
    core = lax.rem(b, 2)
    x, z_lo = p // 2, lax.rem(p, 2)
    x_odd = lax.rem(x, 2) == 1
    even = lax.rem(j, 2) == 0

    px_peer = [(j + k) % N_PX for k in range(N_PX)]
    px_id = [(b, p, t) for t in px_peer]
    py_id = [(b, lax.rem(x + dx, 4) * 2 + (z_lo if dz == 0 else 1 - z_lo), j) for dx, dz in SLOTS]
    core_id = (b + 1 - 2 * core, p, j)
    across_id = (lax.rem(b + jnp.where(z_lo == 1, 2, 6), 8), p + 1 - 2 * z_lo, j)
    x_pair_id = (b, p + 2 - 4 * lax.rem(x, 2), j)

    own_slot = jnp.where(even, 0, 2)
    kind_own = jnp.where(j == 0, 0, jnp.where(j == 3, 2, 1))
    loads = [
        pltpu.make_async_copy(src, dst, load_s.at[i])
        for i, (src, dst) in enumerate(
            (
                (sk_hbm, sk_ref), (sv_hbm, sv_ref), (lat_hbm, lat_ref), (pw_hbm, pw_ref),
                (qw_hbm.at[pl.ds(pl.multiple_of(own_slot * COLS, 16), COLS)], wq.at[kind_own]),
            )
        )
    ]
    for load in loads:
        load.start()

    barrier = pltpu.get_barrier_semaphore()
    peers = px_id[1:] + py_id[1:] + [core_id, across_id]
    for peer in peers:
        pl.semaphore_signal(barrier, inc=1, device_id=peer, device_id_type=MESH)

    loads[0].wait()
    loads[1].wait()
    for t in range(N_PX):
        for h in range(GROUP_HEADS):
            lanes = slice((t * GROUP_HEADS + h) * HEAD_DIM, (t * GROUP_HEADS + h + 1) * HEAD_DIM)
            kvs[t, :, h * 128 : (h + 1) * 128] = jnp.concatenate(
                [sk_ref[:, lanes], sv_ref[:, lanes]], axis=1
            )
    kvg[0, j] = kvs[j]

    pl.semaphore_wait(barrier, len(peers))

    sends = []

    def send(src, dst, r_sem, peer):
        copy = pltpu.make_async_remote_copy(
            src_ref=src, dst_ref=dst, send_sem=send_s.at[len(sends)], recv_sem=r_sem,
            device_id=peer, device_id_type=MESH,
        )
        copy.start()
        sends.append(copy)

    def received(dst, r_sem):
        pltpu.make_async_remote_copy(
            src_ref=dst, dst_ref=dst, send_sem=send_s.at[0], recv_sem=r_sem,
            device_id=px_id[1], device_id_type=MESH,
        ).wait_recv()

    halves = (pl.ds(0, TOK // 2), pl.ds(TOK // 2, TOK // 2))

    kv_done = set()

    def kv_received(slot, k):
        if (slot, k) not in kv_done:
            kv_done.add((slot, k))
            received(kvg.at[slot, px_peer[k]], kv_r.at[slot, px_peer[k]])

    def kv_send(slot, k, to_slot, peer):
        u = px_peer[k]
        send(kvg.at[slot, u], kvg.at[to_slot, u], kv_r.at[to_slot, u], peer)

    def kv_sides(z, k):
        for dx in (1, 3):
            kv_send(z, k, slot_of(-dx, z), py_id[slot_of(dx, 0)])

    def kv_first(k):
        kv_send(0, k, 1, py_id[1])
        kv_sides(0, k)

    def kv_opposite(z, k):
        dx = 3 if k % 2 == 0 else 1
        kv_received(slot_of(dx, z), k)
        kv_send(slot_of(dx, z), k, slot_of(2, z), py_id[slot_of(-dx, 0)])

    def kv_second(k):
        kv_received(1, k)
        kv_sides(1, k)

    def kv_across(dx, k):
        kv_received(slot_of(dx, 0), k)
        kv_send(slot_of(dx, 0), k, slot_of(dx, 1), py_id[1])

    quarter = 2 * z_lo + core
    kind_even = jnp.where(j == 1, 0, jnp.where(j == 2, 2, 1))
    kind_odd = jnp.where(j < 2, 2, 0)
    kind_mine = jnp.where(x_odd, kind_odd, kind_even)
    kind_theirs = jnp.where(x_odd, kind_even, kind_odd)
    target = jnp.where(x_odd, lax.rem(j + 2, 4), j + 1 - 2 * lax.rem(j, 2))
    w_slot = lax.rem(target + j, 4)
    w_kind = (3 * j + w_slot) // 4

    def w_rows(kind, q):
        return wq.at[kind, pl.ds(pl.multiple_of(q * QUARTER, 16), QUARTER)]

    send(
        qw_hbm.at[pl.ds(pl.multiple_of(w_slot * COLS + quarter * QUARTER, 16), QUARTER)],
        w_rows(w_kind, quarter), w_r.at[0], (b, p, target),
    )
    for k in (1, 3):
        send(kvs.at[px_peer[k]], kvg.at[0, j], kv_r.at[0, j], px_id[k])
    kv_first(0)

    for half in range(2):
        for k, own_half in ((1, half), (3, 1 - half)):
            rows = halves[own_half]
            send(lat_hbm.at[rows], latg.at[j, rows], lat_r.at[j, own_half], px_id[k])

    def lat_received(k, half):
        t = px_peer[k]
        received(latg.at[t, halves[half]], lat_r.at[t, half])

    def lat_forward(k, half):
        t = px_peer[k]
        lat_received(k, half)
        rows = halves[half]
        send(latg.at[t, rows], latg.at[t, rows], lat_r.at[t, half], px_id[4 - k])

    chan = lax.broadcasted_iota(jnp.int32, (WIDTH, 128), 0)
    group = lax.broadcasted_iota(jnp.int32, (WIDTH, 128), 1) * (WIDTH // GROUPS)
    member = jnp.where((chan >= group) & (chan < group + WIDTH // GROUPS), 1.0, 0.0).astype(F32)

    def to_groups(row):
        return mm(jnp.broadcast_to(row, (8, WIDTH)), member, HIGHEST)

    def to_channels(row):
        return mm_t(row, member, HIGHEST)[0:1]

    loads[2].wait()
    own = lat_ref[...].astype(F32)
    own_mean = to_groups(jnp.sum(own, axis=0, keepdims=True)) * (1.0 / ENTRIES)
    centered = own - to_channels(own_mean)
    own_squares = to_groups(jnp.sum(centered * centered, axis=0, keepdims=True))
    st_out[0:8] = own_mean
    st_out[8:16] = own_squares
    st_py[0] = st_out[...]
    for i in range(1, 8):
        dx, dz = SLOTS[i]
        send(st_out, st_py.at[slot_of(-dx, dz)], sp_r.at[slot_of(-dx, dz)], py_id[i])

    for i in range(1, 8):
        received(st_py.at[i], sp_r.at[i])
    mean, squares = merge(
        [st_py[i, 0:8] for i in range(8)], [st_py[i, 8:16] for i in range(8)], float(ENTRIES)
    )
    st_mid[0:8] = mean
    st_mid[8:16] = squares
    st_px[j] = st_mid[...]
    for k in range(1, 4):
        send(st_mid, st_px.at[j], sx_r.at[j], px_id[k])
    kv_second(0)
    kv_opposite(0, 0)
    lat_forward(3, 0)
    lat_forward(1, 1)
    send(kvs.at[px_peer[2]], kvg.at[0, j], kv_r.at[0, j], px_id[2])
    received(w_rows(kind_mine, quarter), w_r.at[0])
    send(w_rows(kind_mine, quarter), w_rows(kind_mine, quarter), w_r.at[1], x_pair_id)
    for k in (1, 3):
        kv_received(0, k)
        kv_first(k)
    for k in range(1, 4):
        received(st_px.at[px_peer[k]], sx_r.at[px_peer[k]])
    mean, squares = merge(
        [st_px[i, 0:8] for i in range(4)], [st_px[i, 8:16] for i in range(4)], float(ENTRIES * 8)
    )
    spread_all = squares * (1.0 / (ENTRIES * 32))
    gn_mean = to_channels(mean)
    gn_scale = to_channels(lax.rsqrt(spread_all + 1e-06)) * gng_ref[...].reshape(1, WIDTH)
    gn_shift = gnb_ref[...].reshape(1, WIDTH)

    def own_columns(ref):
        row = ref[...].reshape(1, WIDTH)
        out = row[:, 0:COLS]
        for t in range(1, N_PX):
            out = jnp.where(j == t, row[:, t * COLS : (t + 1) * COLS], out)
        return out

    proj_bias = own_columns(pb_ref)
    ln_gain = own_columns(lng_ref)
    ln_bias = own_columns(lnb_ref)
    lane8 = lax.broadcasted_iota(jnp.int32, (TOK, 8), 1)
    row8 = lax.broadcasted_iota(jnp.int32, (8, TOK), 0)

    def project(t, source):
        grouped = ((source[...].astype(F32) - gn_mean) * gn_scale + gn_shift).astype(BF16)
        out = mm_t(grouped, pw_ref[...]) + proj_bias
        proj[t] = out
        part_mean = jnp.sum(out, axis=1, keepdims=True) * (1.0 / COLS)
        off = out - part_mean
        part_squares = jnp.sum(off * off, axis=1, keepdims=True)
        ln_out[t] = jnp.where(lane8 < 4, part_mean, part_squares).T

    loads[3].wait()
    project(j, lat_ref)
    received(w_rows(kind_theirs, quarter), w_r.at[1])
    for i, kind in enumerate((kind_mine, kind_theirs)):
        send(w_rows(kind, quarter), w_rows(kind, quarter), w_r.at[2 + i], across_id)
    for i, kind in enumerate((kind_mine, kind_theirs)):
        send(w_rows(kind, quarter), w_rows(kind, quarter), w_r.at[4 + i], core_id)
    for k, half in ((3, 1), (1, 0)):
        lat_received(k, half)
        project(px_peer[k], latg.at[px_peer[k]])
    kv_second(1)
    lat_received(2, 0)
    lat_received(2, 1)
    project(px_peer[2], latg.at[px_peer[2]])

    for k in range(1, 4):
        send(ln_out, ln_in.at[j], ln_r.at[j], px_id[k])
    ln_in[j] = ln_out[...]
    kv_received(0, 2)
    kv_first(2)
    for z, k in ((0, 1), (1, 0), (0, 3)):
        kv_opposite(z, k)
    for k in range(1, 4):
        received(ln_in.at[px_peer[k]], ln_r.at[px_peer[k]])
    tails = []
    for t in range(N_PX):
        mean, squares = merge(
            [ln_in[d, t, 0:1] for d in range(N_PX)], [ln_in[d, t, 4:5] for d in range(N_PX)], float(COLS)
        )
        scale = lax.rsqrt(squares * (1.0 / WIDTH) + 1e-05)
        both = jnp.where(row8 < 4, jnp.broadcast_to(mean, (8, TOK)), jnp.broadcast_to(scale, (8, TOK)))
        both = both.T
        normed = ((proj[t] - both[:, 0:1]) * both[:, 4:5] * ln_gain + ln_bias).astype(BF16)
        body = jnp.where(even, normed[:, 0:256], normed[:, HEAD_DIM:])
        tails.append(jnp.where(even, normed[:, 256:], normed[:, 0:HEAD_DIM]))
        for i in range(2):
            start = i * 256 + (t % 2) * TOK
            nrm[j, t // 2, start : start + TOK] = body[:, i * 128 : (i + 1) * 128]
    for half in range(2):
        nrm[j, half, 512:] = jnp.concatenate(tails[2 * half : 2 * half + 2], axis=1)
    for half in range(2):
        for k, own_half in ((1, half), (3, 1 - half)):
            send(nrm.at[j, own_half], nrm.at[j, own_half], nrm_r.at[j, own_half], px_id[k])

    def nrm_received(k, half):
        t = px_peer[k]
        received(nrm.at[t, half], nrm_r.at[t, half])

    def nrm_forward(k, half):
        t = px_peer[k]
        nrm_received(k, half)
        send(nrm.at[t, half], nrm.at[t, half], nrm_r.at[t, half], px_id[4 - k])

    for dx in (1, 3):
        kv_across(dx, 3)
    kv_opposite(0, 2)
    nrm_forward(3, 0)
    nrm_forward(1, 1)
    kv_opposite(1, 1)

    across_q = 2 * (1 - z_lo) + core
    for i, kind in enumerate((kind_mine, kind_theirs)):
        received(w_rows(kind, across_q), w_r.at[2 + i])
        send(w_rows(kind, across_q), w_rows(kind, across_q), w_r.at[6 + i], core_id)
    for dx in (1, 3):
        kv_across(dx, 2)
    for i, kind in enumerate((kind_mine, kind_theirs)):
        received(w_rows(kind, 2 * z_lo + 1 - core), w_r.at[4 + i])
        received(w_rows(kind, 2 * (1 - z_lo) + 1 - core), w_r.at[6 + i])
    loads[4].wait()

    def weight_lanes(start, size):
        return wq[:, :, pl.ds(start, size)].reshape(3 * COLS, size)

    def part(d):
        start = pl.multiple_of((d // 2) * 640 + lax.rem(d, 2) * 384, 128)
        rows = jnp.concatenate(
            [jnp.concatenate([nrm[d, half, 0:256], nrm[d, half, 256:512]], axis=1) for half in range(2)], axis=0
        )
        return mm_t(rows, weight_lanes(start, 256))

    qkv_acc[...] = part(j)
    nrm_received(3, 1)
    qkv_acc[...] += part(px_peer[3])
    nrm_received(1, 0)
    qkv_acc[...] += part(px_peer[1])
    kv_across(2, 3)
    nrm_received(2, 0)
    nrm_received(2, 1)
    qkv_acc[...] += part(px_peer[2])
    tail = jnp.concatenate(
        [
            jnp.concatenate([nrm[d, t // 2, 512:, (t % 2) * 64 : (t % 2) * 64 + 64] for d in range(N_PX)], axis=1)
            for t in range(N_PX)
        ],
        axis=0,
    )
    tail_weight = jnp.concatenate([weight_lanes(256, 128), weight_lanes(896, 128)], axis=1)
    qkv_acc[...] += mm_t(tail, tail_weight)
    blank = jnp.zeros((TOK, HEAD_DIM), BF16)
    for t in range(N_PX):
        rows = qkv_acc[t * TOK : (t + 1) * TOK, :]
        query = (rows[:, 0:COLS] * HEAD_DIM ** (-0.5)).astype(BF16)
        key = rows[:, COLS : 2 * COLS].astype(BF16)
        value = rows[:, 2 * COLS :].astype(BF16)
        for h in range(GROUP_HEADS):
            lanes = slice(h * HEAD_DIM, (h + 1) * HEAD_DIM)
            q_buf[t, :, h * 128 : (h + 1) * 128] = jnp.concatenate([query[:, lanes], blank], axis=1)
            fkv[t, :, h * 128 : (h + 1) * 128] = jnp.concatenate([key[:, lanes], value[:, lanes]], axis=1)
    for k in range(1, 4):
        send(fkv.at[px_peer[k]], fresh_out.at[j], fr_r.at[j], px_id[k])
    keep_fresh = pltpu.make_async_copy(fkv.at[j], fresh_out.at[j], load_s.at[5])
    keep_fresh.start()

    kv_across(2, 2)
    for i in range(1, 4):
        for k in range(N_PX):
            kv_received(i, k)
    lane = lax.broadcasted_iota(jnp.int32, (2048, 128), 1)

    def head_lanes(h):
        return slice(h * 128, (h + 1) * 128)

    def first_keys(h, t):
        lanes = head_lanes(h)
        parts = [fkv[t, :, lanes] if u == t else kvg[0, u, :, lanes] for u in range(N_PX)]
        parts.append(kvg[1:4, :, :, lanes].reshape(1536, 128))
        return jnp.concatenate(parts, axis=0)

    def second_keys(h, t):
        return kvg[4:8, :, :, head_lanes(h)].reshape(2048, 128)

    def weigh(weight, keys):
        return mm(weight.astype(BF16), jnp.where(lane < HEAD_DIM, jnp.ones((), BF16), keys))

    items = [(h, t) for t in range(N_PX) for h in range(GROUP_HEADS)]
    score = mm_t(q_buf[items[0][1], :, head_lanes(items[0][0])], first_keys(*items[0]))
    for n, (h, t) in enumerate(items):
        following = None
        if n + 1 < len(items):
            h2, t2 = items[n + 1]
            following = mm_t(q_buf[t2, :, head_lanes(h2)], first_keys(h2, t2))
        new = jnp.max(score, axis=1, keepdims=True)
        weight = jnp.exp(score - new)
        top[h, t] = jnp.broadcast_to(new, (TOK, 128))
        acc[h, t] = weigh(weight, first_keys(h, t))
        score = following

    for i in range(4, 8):
        for k in range(N_PX):
            kv_received(i, k)
    order = [px_peer[1], px_peer[2], px_peer[3], j]
    items = [(h, k) for k in range(N_PX) for h in range(GROUP_HEADS)]
    score = mm_t(q_buf[order[0], :, head_lanes(0)], second_keys(0, 0))
    outs = []
    for n, (h, k) in enumerate(items):
        following = None
        if n + 1 < len(items):
            h2, k2 = items[n + 1]
            following = mm_t(q_buf[order[k2], :, head_lanes(h2)], second_keys(h2, k2))
        t = order[k]
        old = top[h, t]
        new = jnp.maximum(old, jnp.max(score, axis=1, keepdims=True))
        weight = jnp.exp(score - new[:, 0:1])
        total = acc[h, t] * jnp.exp(old - new) + weigh(weight, second_keys(h, k))
        outs.append(total[:, HEAD_DIM:] / total[:, 0:HEAD_DIM])
        if h == GROUP_HEADS - 1:
            outs.append(jnp.zeros((TOK, HEAD_DIM), F32))
            ost[k] = jnp.concatenate(outs, axis=1).astype(BF16)
            outs = []
            if k < 3:
                send(ost.at[k], att_out.at[j], or_r.at[j], px_id[k + 1])
        score = following

    keep_att = pltpu.make_async_copy(ost.at[3], att_out.at[j], load_s.at[6])
    keep_att.start()
    for k in range(1, 4):
        received(fresh_out.at[px_peer[k]], fr_r.at[px_peer[k]])
    for k in range(1, 4):
        received(att_out.at[px_peer[k]], or_r.at[px_peer[k]])
    keep_fresh.wait()
    keep_att.wait()
    for copy in sends:
        copy.wait_send()


def lay_out(fresh_ref, att_in_ref, att_ref, fk_ref, fv_ref):
    for first, out_ref in ((0, fk_ref), (HEAD_DIM, fv_ref)):
        out_ref[...] = jnp.concatenate(
            [
                fresh_ref[g, :, h * 128 + first : h * 128 + first + HEAD_DIM]
                for g in range(N_PX)
                for h in range(GROUP_HEADS)
            ],
            axis=1,
        )
    att_ref[...] = jnp.concatenate([att_in_ref[g, :, 0:COLS] for g in range(N_PX)], axis=1)


def shards(
    latents, gn_gain, gn_bias, proj_weight, proj_bias, ln_gain, ln_bias, qkv_weight, stale_keys, stale_values
):
    patch_rows, patch_cols, width = latents.shape
    tokens = patch_rows * patch_cols
    dma = pltpu.SemaphoreType.DMA
    vmem = pl.BlockSpec(memory_space=pltpu.VMEM)
    hbm = pl.BlockSpec(memory_space=pl.ANY)
    out = jax.ShapeDtypeStruct((tokens, width), BF16)
    scratch = [
        pltpu.VMEM((TOK, WIDTH), BF16),
        pltpu.VMEM((TOK, WIDTH), BF16),
        pltpu.VMEM((TOK, WIDTH), BF16),
        pltpu.VMEM((COLS, WIDTH), BF16),
        pltpu.VMEM((N_PX, TOK, WIDTH), BF16),
        pltpu.VMEM((16, 128), F32),
        pltpu.VMEM((N_PY, 16, 128), F32),
        pltpu.VMEM((16, 128), F32),
        pltpu.VMEM((N_PX, 16, 128), F32),
        pltpu.VMEM((N_PX, TOK, COLS), F32),
        pltpu.VMEM((N_PX, 8, TOK), F32),
        pltpu.VMEM((N_PX, N_PX, 8, TOK), F32),
        pltpu.VMEM((N_PX, 2, 640, 128), BF16),
        pltpu.VMEM((3, COLS, WIDTH), BF16),
        pltpu.VMEM((4 * TOK, 3 * COLS), F32),
        pltpu.VMEM((N_PX, TOK, PAIR), BF16),
        pltpu.VMEM((N_PX, TOK, PAIR), BF16),
        pltpu.VMEM((N_PX, TOK, PAIR), BF16),
        pltpu.VMEM((N_PY, N_PX, TOK, PAIR), BF16),
        pltpu.VMEM((GROUP_HEADS, N_PX, TOK, 128), F32),
        pltpu.VMEM((GROUP_HEADS, N_PX, TOK, 128), F32),
        pltpu.VMEM((N_PX, TOK, 384), BF16),
    ]
    sems = [(7,), (80,), (4, 2), (8,), (4,), (4,), (4, 2), (8,), (8, 4), (4,), (4,)]
    fresh, groups = pl.pallas_call(
        kernel,
        out_shape=(
            jax.ShapeDtypeStruct((N_PX, TOK, PAIR), BF16),
            jax.ShapeDtypeStruct((N_PX, TOK, 384), BF16),
        ),
        in_specs=[hbm, vmem, vmem, hbm, vmem, vmem, vmem, hbm, hbm, hbm],
        out_specs=(hbm, hbm),
        scratch_shapes=scratch + [dma(shape) for shape in sems],
        compiler_params=pltpu.CompilerParams(
            collective_id=0, has_side_effects=True, vmem_limit_bytes=56 * 1024 * 1024
        ),
        name="patch_attention",
    )(
        latents.reshape(tokens, width),
        gn_gain, gn_bias, proj_weight.T, proj_bias, ln_gain, ln_bias, qkv_weight.T,
        stale_keys.reshape(tokens, width), stale_values.reshape(tokens, width),
    )
    attended, fresh_keys, fresh_values = pl.pallas_call(
        lay_out,
        out_shape=(out, out, out),
        in_specs=[vmem, vmem],
        out_specs=(vmem, vmem, vmem),
        name="lay_out",
    )(fresh, groups)
    shape = (patch_rows, patch_cols, width)
    return attended.reshape(shape), fresh_keys.reshape(shape), fresh_values.reshape(shape)


def solution(mesh):
    split = P(("batch", "py"), "px", None)
    return jax.shard_map(
        shards,
        mesh=mesh,
        in_specs=(split, P(), P(), P(None, "px"), P(), P(), P(), P(None, "px"), split, split),
        out_specs=(split, split, split),
        check_vma=False,
    )
```

```python
import jax
import jax.numpy as jnp
from jax import lax
from jax.experimental import pallas as pl
from jax.experimental.pallas import tpu as pltpu
from jax.sharding import PartitionSpec as P

MESH = pl.DeviceIdType.MESH
HIGHEST = lax.Precision.HIGHEST
BF16 = jnp.bfloat16
F32 = jnp.float32

WIDTH = 1280
HEADS = 20
HEAD_DIM = 64
GROUPS = 32
N_PY = 8
N_PX = 4
TOK = 128
GROUP_HEADS = HEADS // N_PX
COLS = WIDTH // N_PX
QUARTER = COLS // 4
PAIR = GROUP_HEADS * 2 * HEAD_DIM
ENTRIES = TOK * (WIDTH // GROUPS)

SLOTS = ((0, 0), (0, 1), (1, 0), (3, 0), (1, 1), (3, 1), (2, 0), (2, 1))


def slot_of(dx, dz):
    return SLOTS.index((dx % 4, dz))


def mm(a, b, precision=None):
    return lax.dot_general(
        a, b, (((1,), (0,)), ((), ())), precision=precision, preferred_element_type=F32
    )


def mm_t(a, b, precision=None):
    return lax.dot_general(
        a, b, (((1,), (1,)), ((), ())), precision=precision, preferred_element_type=F32
    )


def merge(means, squares, count):
    n = len(means)
    mean = sum(means[1:], means[0]) * (1.0 / n)
    total = sum(squares[1:], squares[0])
    for part in means:
        total = total + count * (part - mean) * (part - mean)
    return mean, total


def kernel(
    lat_hbm, gng_ref, gnb_ref, pw_hbm, pb_ref, lng_ref, lnb_ref, qw_hbm, sk_hbm, sv_hbm,
    fresh_out, att_out,
    lat_ref, sk_ref, sv_ref, pw_ref, latg, st_out, st_py, st_mid, st_px, proj, ln_out, ln_in, nrm,
    wq, qkv_acc, q_buf, fkv, kvs, kvg, acc, top, ost,
    load_s, send_s, lat_r, sp_r, sx_r, ln_r, nrm_r, w_r, kv_r, fr_r, or_r,
):
    b = lax.axis_index("batch")
    p = lax.axis_index("py")
    j = lax.axis_index("px")
    core = lax.rem(b, 2)
    x, z_lo = p // 2, lax.rem(p, 2)
    x_odd = lax.rem(x, 2) == 1
    even = lax.rem(j, 2) == 0

    px_peer = [(j + k) % N_PX for k in range(N_PX)]
    px_id = [(b, p, t) for t in px_peer]
    py_id = [(b, lax.rem(x + dx, 4) * 2 + (z_lo if dz == 0 else 1 - z_lo), j) for dx, dz in SLOTS]
    core_id = (b + 1 - 2 * core, p, j)
    across_id = (lax.rem(b + jnp.where(z_lo == 1, 2, 6), 8), p + 1 - 2 * z_lo, j)
    x_pair_id = (b, p + 2 - 4 * lax.rem(x, 2), j)

    own_slot = jnp.where(even, 0, 2)
    kind_own = jnp.where(j == 0, 0, jnp.where(j == 3, 2, 1))
    loads = [
        pltpu.make_async_copy(src, dst, load_s.at[i])
        for i, (src, dst) in enumerate(
            (
                (sk_hbm, sk_ref), (sv_hbm, sv_ref), (lat_hbm, lat_ref), (pw_hbm, pw_ref),
                (qw_hbm.at[pl.ds(pl.multiple_of(own_slot * COLS, 16), COLS)], wq.at[kind_own]),
            )
        )
    ]
    for load in loads:
        load.start()

    barrier = pltpu.get_barrier_semaphore()
    peers = px_id[1:] + py_id[1:] + [core_id, across_id]
    for peer in peers:
        pl.semaphore_signal(barrier, inc=1, device_id=peer, device_id_type=MESH)

    loads[0].wait()
    loads[1].wait()
    for t in range(N_PX):
        for h in range(GROUP_HEADS):
            lanes = slice((t * GROUP_HEADS + h) * HEAD_DIM, (t * GROUP_HEADS + h + 1) * HEAD_DIM)
            kvs[t, :, h * 128 : (h + 1) * 128] = jnp.concatenate(
                [sk_ref[:, lanes], sv_ref[:, lanes]], axis=1
            )
    kvg[0, j] = kvs[j]

    pl.semaphore_wait(barrier, len(peers))

    sends = []

    def send(src, dst, r_sem, peer):
        copy = pltpu.make_async_remote_copy(
            src_ref=src, dst_ref=dst, send_sem=send_s.at[len(sends)], recv_sem=r_sem,
            device_id=peer, device_id_type=MESH,
        )
        copy.start()
        sends.append(copy)

    def received(dst, r_sem):
        pltpu.make_async_remote_copy(
            src_ref=dst, dst_ref=dst, send_sem=send_s.at[0], recv_sem=r_sem,
            device_id=px_id[1], device_id_type=MESH,
        ).wait_recv()

    halves = (pl.ds(0, TOK // 2), pl.ds(TOK // 2, TOK // 2))

    kv_done = set()

    def kv_received(slot, k):
        if (slot, k) not in kv_done:
            kv_done.add((slot, k))
            received(kvg.at[slot, px_peer[k]], kv_r.at[slot, px_peer[k]])

    def kv_send(slot, k, to_slot, peer):
        u = px_peer[k]
        send(kvg.at[slot, u], kvg.at[to_slot, u], kv_r.at[to_slot, u], peer)

    def kv_sides(z, k):
        for dx in (1, 3):
            kv_send(z, k, slot_of(-dx, z), py_id[slot_of(dx, 0)])

    def kv_first(k):
        kv_send(0, k, 1, py_id[1])
        kv_sides(0, k)

    def kv_opposite(z, k):
        dx = 3 if k % 2 == 0 else 1
        kv_received(slot_of(dx, z), k)
        kv_send(slot_of(dx, z), k, slot_of(2, z), py_id[slot_of(-dx, 0)])

    def kv_second(k):
        kv_received(1, k)
        kv_sides(1, k)

    def kv_across(dx, k):
        kv_received(slot_of(dx, 0), k)
        kv_send(slot_of(dx, 0), k, slot_of(dx, 1), py_id[1])

    quarter = 2 * z_lo + core
    kind_even = jnp.where(j == 1, 0, jnp.where(j == 2, 2, 1))
    kind_odd = jnp.where(j < 2, 2, 0)
    kind_mine = jnp.where(x_odd, kind_odd, kind_even)
    kind_theirs = jnp.where(x_odd, kind_even, kind_odd)
    target = jnp.where(x_odd, lax.rem(j + 2, 4), j + 1 - 2 * lax.rem(j, 2))
    w_slot = lax.rem(target + j, 4)
    w_kind = (3 * j + w_slot) // 4

    def w_rows(kind, q):
        return wq.at[kind, pl.ds(pl.multiple_of(q * QUARTER, 16), QUARTER)]

    send(
        qw_hbm.at[pl.ds(pl.multiple_of(w_slot * COLS + quarter * QUARTER, 16), QUARTER)],
        w_rows(w_kind, quarter), w_r.at[0], (b, p, target),
    )
    for k in (1, 3):
        send(kvs.at[px_peer[k]], kvg.at[0, j], kv_r.at[0, j], px_id[k])
    kv_first(0)

    for half in range(2):
        for k, own_half in ((1, half), (3, 1 - half)):
            rows = halves[own_half]
            send(lat_hbm.at[rows], latg.at[j, rows], lat_r.at[j, own_half], px_id[k])

    def lat_received(k, half):
        t = px_peer[k]
        received(latg.at[t, halves[half]], lat_r.at[t, half])

    def lat_forward(k, half):
        t = px_peer[k]
        lat_received(k, half)
        rows = halves[half]
        send(latg.at[t, rows], latg.at[t, rows], lat_r.at[t, half], px_id[4 - k])

    chan = lax.broadcasted_iota(jnp.int32, (WIDTH, 128), 0)
    group = lax.broadcasted_iota(jnp.int32, (WIDTH, 128), 1) * (WIDTH // GROUPS)
    member = jnp.where((chan >= group) & (chan < group + WIDTH // GROUPS), 1.0, 0.0).astype(F32)

    def to_groups(row):
        return mm(jnp.broadcast_to(row, (8, WIDTH)), member, HIGHEST)

    def to_channels(row):
        return mm_t(row, member, HIGHEST)[0:1]

    loads[2].wait()
    own = lat_ref[...].astype(F32)
    own_mean = to_groups(jnp.sum(own, axis=0, keepdims=True)) * (1.0 / ENTRIES)
    centered = own - to_channels(own_mean)
    own_squares = to_groups(jnp.sum(centered * centered, axis=0, keepdims=True))
    st_out[0:8] = own_mean
    st_out[8:16] = own_squares
    st_py[0] = st_out[...]
    for i in range(1, 8):
        dx, dz = SLOTS[i]
        send(st_out, st_py.at[slot_of(-dx, dz)], sp_r.at[slot_of(-dx, dz)], py_id[i])

    for i in range(1, 8):
        received(st_py.at[i], sp_r.at[i])
    mean, squares = merge(
        [st_py[i, 0:8] for i in range(8)], [st_py[i, 8:16] for i in range(8)], float(ENTRIES)
    )
    st_mid[0:8] = mean
    st_mid[8:16] = squares
    st_px[j] = st_mid[...]
    for k in range(1, 4):
        send(st_mid, st_px.at[j], sx_r.at[j], px_id[k])
    kv_second(0)
    kv_opposite(0, 0)
    lat_forward(3, 0)
    lat_forward(1, 1)
    send(kvs.at[px_peer[2]], kvg.at[0, j], kv_r.at[0, j], px_id[2])
    received(w_rows(kind_mine, quarter), w_r.at[0])
    send(w_rows(kind_mine, quarter), w_rows(kind_mine, quarter), w_r.at[1], x_pair_id)
    for k in (1, 3):
        kv_received(0, k)
        kv_first(k)
    for k in range(1, 4):
        received(st_px.at[px_peer[k]], sx_r.at[px_peer[k]])
    mean, squares = merge(
        [st_px[i, 0:8] for i in range(4)], [st_px[i, 8:16] for i in range(4)], float(ENTRIES * 8)
    )
    spread_all = squares * (1.0 / (ENTRIES * 32))
    gn_mean = to_channels(mean)
    gn_scale = to_channels(lax.rsqrt(spread_all + 1e-06)) * gng_ref[...].reshape(1, WIDTH)
    gn_shift = gnb_ref[...].reshape(1, WIDTH)

    def own_columns(ref):
        row = ref[...].reshape(1, WIDTH)
        out = row[:, 0:COLS]
        for t in range(1, N_PX):
            out = jnp.where(j == t, row[:, t * COLS : (t + 1) * COLS], out)
        return out

    proj_bias = own_columns(pb_ref)
    ln_gain = own_columns(lng_ref)
    ln_bias = own_columns(lnb_ref)
    lane8 = lax.broadcasted_iota(jnp.int32, (TOK, 8), 1)
    row8 = lax.broadcasted_iota(jnp.int32, (8, TOK), 0)

    def project(t, source):
        grouped = ((source[...].astype(F32) - gn_mean) * gn_scale + gn_shift).astype(BF16)
        out = mm_t(grouped, pw_ref[...]) + proj_bias
        proj[t] = out
        part_mean = jnp.sum(out, axis=1, keepdims=True) * (1.0 / COLS)
        off = out - part_mean
        part_squares = jnp.sum(off * off, axis=1, keepdims=True)
        ln_out[t] = jnp.where(lane8 < 4, part_mean, part_squares).T

    loads[3].wait()
    project(j, lat_ref)
    received(w_rows(kind_theirs, quarter), w_r.at[1])
    for i, kind in enumerate((kind_mine, kind_theirs)):
        send(w_rows(kind, quarter), w_rows(kind, quarter), w_r.at[2 + i], across_id)
    for i, kind in enumerate((kind_mine, kind_theirs)):
        send(w_rows(kind, quarter), w_rows(kind, quarter), w_r.at[4 + i], core_id)
    for k, half in ((3, 1), (1, 0)):
        lat_received(k, half)
        project(px_peer[k], latg.at[px_peer[k]])
    kv_second(1)
    lat_received(2, 0)
    lat_received(2, 1)
    project(px_peer[2], latg.at[px_peer[2]])

    for k in range(1, 4):
        send(ln_out, ln_in.at[j], ln_r.at[j], px_id[k])
    ln_in[j] = ln_out[...]
    kv_received(0, 2)
    kv_first(2)
    for z, k in ((0, 1), (1, 0), (0, 3)):
        kv_opposite(z, k)
    for k in range(1, 4):
        received(ln_in.at[px_peer[k]], ln_r.at[px_peer[k]])
    tails = []
    for t in range(N_PX):
        mean, squares = merge(
            [ln_in[d, t, 0:1] for d in range(N_PX)], [ln_in[d, t, 4:5] for d in range(N_PX)], float(COLS)
        )
        scale = lax.rsqrt(squares * (1.0 / WIDTH) + 1e-05)
        both = jnp.where(row8 < 4, jnp.broadcast_to(mean, (8, TOK)), jnp.broadcast_to(scale, (8, TOK)))
        both = both.T
        normed = ((proj[t] - both[:, 0:1]) * both[:, 4:5] * ln_gain + ln_bias).astype(BF16)
        body = jnp.where(even, normed[:, 0:256], normed[:, HEAD_DIM:])
        tails.append(jnp.where(even, normed[:, 256:], normed[:, 0:HEAD_DIM]))
        for i in range(2):
            start = i * 256 + (t % 2) * TOK
            nrm[j, t // 2, start : start + TOK] = body[:, i * 128 : (i + 1) * 128]
    for half in range(2):
        nrm[j, half, 512:] = jnp.concatenate(tails[2 * half : 2 * half + 2], axis=1)
    for half in range(2):
        for k, own_half in ((1, half), (3, 1 - half)):
            send(nrm.at[j, own_half], nrm.at[j, own_half], nrm_r.at[j, own_half], px_id[k])

    def nrm_received(k, half):
        t = px_peer[k]
        received(nrm.at[t, half], nrm_r.at[t, half])

    def nrm_forward(k, half):
        t = px_peer[k]
        nrm_received(k, half)
        send(nrm.at[t, half], nrm.at[t, half], nrm_r.at[t, half], px_id[4 - k])

    for dx in (1, 3):
        kv_across(dx, 3)
    kv_opposite(0, 2)
    nrm_forward(3, 0)
    nrm_forward(1, 1)
    kv_opposite(1, 1)

    across_q = 2 * (1 - z_lo) + core
    for i, kind in enumerate((kind_mine, kind_theirs)):
        received(w_rows(kind, across_q), w_r.at[2 + i])
        send(w_rows(kind, across_q), w_rows(kind, across_q), w_r.at[6 + i], core_id)
    for dx in (1, 3):
        kv_across(dx, 2)
    for i, kind in enumerate((kind_mine, kind_theirs)):
        received(w_rows(kind, 2 * z_lo + 1 - core), w_r.at[4 + i])
        received(w_rows(kind, 2 * (1 - z_lo) + 1 - core), w_r.at[6 + i])
    loads[4].wait()

    def weight_lanes(start, size):
        return wq[:, :, pl.ds(start, size)].reshape(3 * COLS, size)

    def part(d):
        start = pl.multiple_of((d // 2) * 640 + lax.rem(d, 2) * 384, 128)
        rows = jnp.concatenate(
            [jnp.concatenate([nrm[d, half, 0:256], nrm[d, half, 256:512]], axis=1) for half in range(2)], axis=0
        )
        return mm_t(rows, weight_lanes(start, 256))

    qkv_acc[...] = part(j)
    nrm_received(3, 1)
    qkv_acc[...] += part(px_peer[3])
    nrm_received(1, 0)
    qkv_acc[...] += part(px_peer[1])
    kv_across(2, 3)
    nrm_received(2, 0)
    nrm_received(2, 1)
    qkv_acc[...] += part(px_peer[2])
    tail = jnp.concatenate(
        [
            jnp.concatenate([nrm[d, t // 2, 512:, (t % 2) * 64 : (t % 2) * 64 + 64] for d in range(N_PX)], axis=1)
            for t in range(N_PX)
        ],
        axis=0,
    )
    tail_weight = jnp.concatenate([weight_lanes(256, 128), weight_lanes(896, 128)], axis=1)
    qkv_acc[...] += mm_t(tail, tail_weight)
    blank = jnp.zeros((TOK, HEAD_DIM), BF16)
    for t in range(N_PX):
        rows = qkv_acc[t * TOK : (t + 1) * TOK, :]
        query = (rows[:, 0:COLS] * HEAD_DIM ** (-0.5)).astype(BF16)
        key = rows[:, COLS : 2 * COLS].astype(BF16)
        value = rows[:, 2 * COLS :].astype(BF16)
        for h in range(GROUP_HEADS):
            lanes = slice(h * HEAD_DIM, (h + 1) * HEAD_DIM)
            q_buf[t, :, h * 128 : (h + 1) * 128] = jnp.concatenate([query[:, lanes], blank], axis=1)
            fkv[t, :, h * 128 : (h + 1) * 128] = jnp.concatenate([key[:, lanes], value[:, lanes]], axis=1)
    for k in range(1, 4):
        send(fkv.at[px_peer[k]], fresh_out.at[j], fr_r.at[j], px_id[k])
    keep_fresh = pltpu.make_async_copy(fkv.at[j], fresh_out.at[j], load_s.at[5])
    keep_fresh.start()

    for i in range(1, 4):
        for k in range(N_PX):
            kv_received(i, k)
    lane = lax.broadcasted_iota(jnp.int32, (2048, 128), 1)

    def head_lanes(h):
        return slice(h * 128, (h + 1) * 128)

    def first_keys(h, t):
        lanes = head_lanes(h)
        parts = [fkv[t, :, lanes] if u == t else kvg[0, u, :, lanes] for u in range(N_PX)]
        parts.append(kvg[1:4, :, :, lanes].reshape(1536, 128))
        return jnp.concatenate(parts, axis=0)

    def second_keys(h, t):
        return kvg[4:8, :, :, head_lanes(h)].reshape(2048, 128)

    def weigh(weight, keys):
        return mm(weight.astype(BF16), jnp.where(lane < HEAD_DIM, jnp.ones((), BF16), keys))

    items = [(h, t) for t in range(N_PX) for h in range(GROUP_HEADS)]
    score = mm_t(q_buf[items[0][1], :, head_lanes(items[0][0])], first_keys(*items[0]))
    for n, (h, t) in enumerate(items):
        following = None
        if n + 1 < len(items):
            h2, t2 = items[n + 1]
            following = mm_t(q_buf[t2, :, head_lanes(h2)], first_keys(h2, t2))
        if n == len(items) // 2:
            kv_across(2, 2)
        new = jnp.max(score, axis=1, keepdims=True)
        weight = jnp.exp(score - new)
        top[h, t] = jnp.broadcast_to(new, (TOK, 128))
        acc[h, t] = weigh(weight, first_keys(h, t))
        score = following

    for i in range(4, 8):
        for k in range(N_PX):
            kv_received(i, k)
    order = [px_peer[1], px_peer[2], px_peer[3], j]
    items = [(h, k) for k in range(N_PX) for h in range(GROUP_HEADS)]
    score = mm_t(q_buf[order[0], :, head_lanes(0)], second_keys(0, 0))
    outs = []
    for n, (h, k) in enumerate(items):
        following = None
        if n + 1 < len(items):
            h2, k2 = items[n + 1]
            following = mm_t(q_buf[order[k2], :, head_lanes(h2)], second_keys(h2, k2))
        t = order[k]
        old = top[h, t]
        new = jnp.maximum(old, jnp.max(score, axis=1, keepdims=True))
        weight = jnp.exp(score - new[:, 0:1])
        total = acc[h, t] * jnp.exp(old - new) + weigh(weight, second_keys(h, k))
        outs.append(total[:, HEAD_DIM:] / total[:, 0:HEAD_DIM])
        if h == GROUP_HEADS - 1:
            outs.append(jnp.zeros((TOK, HEAD_DIM), F32))
            ost[k] = jnp.concatenate(outs, axis=1).astype(BF16)
            outs = []
            if k < 3:
                send(ost.at[k], att_out.at[j], or_r.at[j], px_id[k + 1])
        score = following

    keep_att = pltpu.make_async_copy(ost.at[3], att_out.at[j], load_s.at[6])
    keep_att.start()
    for k in range(1, 4):
        received(fresh_out.at[px_peer[k]], fr_r.at[px_peer[k]])
    for k in range(1, 4):
        received(att_out.at[px_peer[k]], or_r.at[px_peer[k]])
    keep_fresh.wait()
    keep_att.wait()
    for copy in sends:
        copy.wait_send()


def lay_out(fresh_ref, att_in_ref, att_ref, fk_ref, fv_ref):
    for first, out_ref in ((0, fk_ref), (HEAD_DIM, fv_ref)):
        out_ref[...] = jnp.concatenate(
            [
                fresh_ref[g, :, h * 128 + first : h * 128 + first + HEAD_DIM]
                for g in range(N_PX)
                for h in range(GROUP_HEADS)
            ],
            axis=1,
        )
    att_ref[...] = jnp.concatenate([att_in_ref[g, :, 0:COLS] for g in range(N_PX)], axis=1)


def shards(
    latents, gn_gain, gn_bias, proj_weight, proj_bias, ln_gain, ln_bias, qkv_weight, stale_keys, stale_values
):
    patch_rows, patch_cols, width = latents.shape
    tokens = patch_rows * patch_cols
    dma = pltpu.SemaphoreType.DMA
    vmem = pl.BlockSpec(memory_space=pltpu.VMEM)
    hbm = pl.BlockSpec(memory_space=pl.ANY)
    out = jax.ShapeDtypeStruct((tokens, width), BF16)
    scratch = [
        pltpu.VMEM((TOK, WIDTH), BF16),
        pltpu.VMEM((TOK, WIDTH), BF16),
        pltpu.VMEM((TOK, WIDTH), BF16),
        pltpu.VMEM((COLS, WIDTH), BF16),
        pltpu.VMEM((N_PX, TOK, WIDTH), BF16),
        pltpu.VMEM((16, 128), F32),
        pltpu.VMEM((N_PY, 16, 128), F32),
        pltpu.VMEM((16, 128), F32),
        pltpu.VMEM((N_PX, 16, 128), F32),
        pltpu.VMEM((N_PX, TOK, COLS), F32),
        pltpu.VMEM((N_PX, 8, TOK), F32),
        pltpu.VMEM((N_PX, N_PX, 8, TOK), F32),
        pltpu.VMEM((N_PX, 2, 640, 128), BF16),
        pltpu.VMEM((3, COLS, WIDTH), BF16),
        pltpu.VMEM((4 * TOK, 3 * COLS), F32),
        pltpu.VMEM((N_PX, TOK, PAIR), BF16),
        pltpu.VMEM((N_PX, TOK, PAIR), BF16),
        pltpu.VMEM((N_PX, TOK, PAIR), BF16),
        pltpu.VMEM((N_PY, N_PX, TOK, PAIR), BF16),
        pltpu.VMEM((GROUP_HEADS, N_PX, TOK, 128), F32),
        pltpu.VMEM((GROUP_HEADS, N_PX, TOK, 128), F32),
        pltpu.VMEM((N_PX, TOK, 384), BF16),
    ]
    sems = [(7,), (80,), (4, 2), (8,), (4,), (4,), (4, 2), (8,), (8, 4), (4,), (4,)]
    fresh, groups = pl.pallas_call(
        kernel,
        out_shape=(
            jax.ShapeDtypeStruct((N_PX, TOK, PAIR), BF16),
            jax.ShapeDtypeStruct((N_PX, TOK, 384), BF16),
        ),
        in_specs=[hbm, vmem, vmem, hbm, vmem, vmem, vmem, hbm, hbm, hbm],
        out_specs=(hbm, hbm),
        scratch_shapes=scratch + [dma(shape) for shape in sems],
        compiler_params=pltpu.CompilerParams(
            collective_id=0, has_side_effects=True, vmem_limit_bytes=56 * 1024 * 1024
        ),
        name="patch_attention",
    )(
        latents.reshape(tokens, width),
        gn_gain, gn_bias, proj_weight.T, proj_bias, ln_gain, ln_bias, qkv_weight.T,
        stale_keys.reshape(tokens, width), stale_values.reshape(tokens, width),
    )
    attended, fresh_keys, fresh_values = pl.pallas_call(
        lay_out,
        out_shape=(out, out, out),
        in_specs=[vmem, vmem],
        out_specs=(vmem, vmem, vmem),
        name="lay_out",
    )(fresh, groups)
    shape = (patch_rows, patch_cols, width)
    return attended.reshape(shape), fresh_keys.reshape(shape), fresh_values.reshape(shape)


def solution(mesh):
    split = P(("batch", "py"), "px", None)
    return jax.shard_map(
        shards,
        mesh=mesh,
        in_specs=(split, P(), P(), P(None, "px"), P(), P(), P(), P(None, "px"), split, split),
        out_specs=(split, split, split),
        check_vma=False,
    )
```
